128 devices in a mesh: member: 8 (over y, core), lon: 16 (over x, z).
Axes of the slice: x: 4, y: 4, z: 4, core: 2. Of those that a mesh axis runs over, the one named last changes fastest.
Arguments:
- ensemble: float32 [96, 3, 64, 4096], P('member', None, None, 'lon')
- perturbation: float32 [96, 3, 64, 4096], P('member', None, None, 'lon'), may hold values from -2.4 to 2.4
- observed: float32 [64, 4096], P(None, 'lon'), may hold values from -6 to 6
- precision: float32 [64, 4096], P(None, 'lon'), may hold values from 0.1 to 1
- nudging: float32 [64, 4096], P(None, 'lon'), may hold values from 0.05 to 0.3
- ancestors: int32 [96], replicated, may hold values from 0 to 95, as said below
Outputs:
- weights: float32 [96], P('member')
- analysis: float32 [96, 3, 64, 4096], P('member', None, None, 'lon')
The draws below stay inside these ranges and needn't reach their ends.
Inputs may be any that keep to these rules, and one draw needn't show every extreme that they name: Number the particles in blocks of 12 (block b holds particles b * 12 to (b + 1) * 12 - 1). Within each block of new particles, at most 3 have ancestors in any one block of old particles, and in every block of new particles some one block of old particles is named exactly 3 times.
All inputs are finite; a program needn't handle non-finite values.
Results may differ from the reference program's by a relative error of at most 0.0003.
Values sent between devices are 32-bit elements; how exact they have to be, the bound alone decides.
A program may use at most 128 MiB of HBM per device.

```python
import math
import jax
import jax.numpy as jnp
from jax import lax

LAT = 64
PART_DEV = 12
CAP = 3
STEPS = 3
NLON = 4096
PARTICLES = 96


def draw_ensemble(key, part):
    key = jax.random.fold_in(key, 11)
    first, second = jax.random.split(key)
    amplitude = jnp.exp(jax.random.uniform(first, (PARTICLES, 1, 1, 1), jnp.float32, jnp.log(0.5), jnp.log(1.5)))
    return amplitude * jax.random.normal(second, (PARTICLES, 3, LAT, NLON), jnp.float32)


def draw_ancestors(key, part):
    key = jax.random.fold_in(key, 23)
    groups = PARTICLES // PART_DEV
    keys = jax.random.split(key, groups)

    def one_block(block_key):
        key_a, key_b, key_c, key_d = jax.random.split(block_key, 4)
        lead_particle = jax.random.randint(key_a, (), 0, groups)
        others = (lead_particle + 1 + jnp.arange(groups - 1, dtype=jnp.int32)) % groups
        pool = jax.random.permutation(key_b, jnp.repeat(others, CAP))
        selected_rows = jnp.concatenate([jnp.full((CAP,), lead_particle, jnp.int32), pool[:PART_DEV - CAP].astype(jnp.int32)])
        selected_rows = jax.random.permutation(key_c, selected_rows)
        within = jax.random.randint(key_d, (PART_DEV,), 0, PART_DEV)
        return selected_rows * PART_DEV + within
    return jax.vmap(one_block)(keys).reshape(PARTICLES).astype(jnp.int32)


def block_scale(rng, shape, cuts, smallest, top_value):
    def one(axis_at, parts):
        steps = jax.random.uniform(jax.random.fold_in(jax.random.fold_in(rng, 6), axis_at), (parts,), jnp.float32, smallest / len(cuts), top_value / len(cuts))
        return jnp.repeat(jnp.exp(steps), shape[axis_at] // parts).reshape((-1,) + (1,) * (len(shape) - axis_at - 1))

    loudness = one(*cuts[0])
    for cut in cuts[1:]:
        loudness = loudness * one(*cut)
    return loudness


def centred(key, dims, deviation, most, shards=(), kind=jnp.bfloat16):
    entries = jax.random.normal(key, dims, jnp.float32) * deviation
    if len(shards) > 0:
        entries = block_scale(key, dims, shards, -0.22, 0.18) * entries
    return jnp.clip(entries, min=-most, max=most).astype(kind)


def setup_inputs(seed: int = 0) -> dict:
    splits = jax.random.split(jax.random.key(seed), 7)
    return {
        "ensemble": draw_ensemble(jax.random.fold_in(splits[6], 71), 0),
        "perturbation": centred(splits[1], (PARTICLES, STEPS, LAT, NLON), 0.3, 2.4, ((0, 8), (3, 16)), jnp.float32),
        "observed": centred(splits[2], (LAT, NLON), 1.0, 6.0, ((1, 16),), jnp.float32),
        "precision": jnp.clip(jnp.exp(math.log(1.0) - 2.3025851 * jax.random.uniform(splits[3], (LAT, NLON), jnp.float32) ** block_scale(splits[3], (LAT, NLON), ((1, 16),), -0.2, 0.2)), 0.1, 1.0),
        "nudging": jnp.clip(jnp.exp(math.log(0.3) - 1.7917595 * jax.random.uniform(splits[4], (LAT, NLON), jnp.float32) ** block_scale(splits[4], (LAT, NLON), ((1, 16),), -0.2, 0.2)), 0.05, 0.3),
        "ancestors": draw_ancestors(jax.random.fold_in(splits[6], 71), 0),
    }


gravity_term = 0.25
depth_term = 0.25


def across(q):
    return (jnp.roll(q, -1, -1) - jnp.roll(q, 1, -1)) * 0.5


def along(q):
    padded = jnp.pad(q, ((1, 1), (0, 0)))
    return (padded[2:] - padded[:-2]) * 0.5


def reference(ensemble, perturbation, observed, precision, nudging, ancestors):
    rows = jnp.arange(LAT).astype(jnp.float32)
    coriolis = (0.3 * jnp.sin(jnp.pi * (rows + 0.5 - LAT / 2) / LAT))[:, None]

    def predicted_state(pair_partner):
        state, forcing = pair_partner
        u, v, h = state[0], state[1], state[2]
        for step in range(STEPS):
            u_new = u + coriolis * v - gravity_term * across(h)
            v_new = v - coriolis * u - gravity_term * along(h)
            h_new = h - depth_term * (across(u_new) + along(v_new)) + nudging * (observed - h) + forcing[step]
            u, v, h = u_new, v_new, h_new
        residual = observed - h
        total = jnp.sum(precision * residual * residual)
        return jnp.stack([u, v, h], axis=0), total

    model_fields, weight_totals = lax.map(predicted_state, (ensemble, perturbation))
    logw = weight_totals * (-2.0 / (LAT * NLON))
    weights = jax.nn.softmax(logw)
    analysis = jnp.take(model_fields, ancestors, axis=0)
    return weights, analysis
```

```python
import functools
import math

import jax
import jax.numpy as jnp
import numpy as np
from jax import lax
from jax.experimental import pallas as pl
from jax.experimental.pallas import tpu as pltpu
from jax.sharding import PartitionSpec as P

MESH = pl.DeviceIdType.MESH
F32 = jnp.float32
STEPS = 3
LAT = 64
CLON = 256
PART = 12
CHIP = 24
HALO = 6
WIN = 18
PER_TILE = 7
FAR = 6
OPEN = 8
CAPACITY = 24
LEVELS = (24,)
SLOTS = CHIP + 2 * CAPACITY
GATHER_AT = 2 * CAPACITY
LEVEL_AT = GATHER_AT + PART


def plan_kernel(anc_ref, plan_ref, need, ranks, lists):
    member = lax.axis_index("member")
    chip = lax.div(member, 2)

    def third(a):
        return lax.shift_right_logical(a * 2731, 16)

    for i in range(4 * 96):
        need[i] = 0
    for j in range(96):
        need[(j // CHIP) * 96 + anc_ref[j]] = 1
    counts = {}
    for d in range(4):
        for k in range(1, 4):
            s = (d + k) % 4
            cnt = jnp.int32(0)
            for p in range(CHIP):
                v = need[d * 96 + s * CHIP + p]
                ranks[d * 96 + s * CHIP + p] = cnt
                lists[(d * 4 + k) * 32 + cnt] = p
                cnt = cnt + v
            counts[d, k] = cnt
    c1 = [counts[d, 1] for d in range(4)]
    c2 = [counts[d, 2] for d in range(4)]
    c3 = [counts[d, 3] for d in range(4)]

    def clamp(d, x):
        return jnp.minimum(jnp.maximum(x, jnp.maximum(0, c2[d] - FAR)), jnp.minimum(FAR, c2[d]))

    def worst(a):
        top = jnp.int32(0)
        for s in range(4):
            d1, d2, u1 = (s - 1) % 4, (s - 2) % 4, (s + 1) % 4
            down = jnp.maximum(OPEN, a[d2] + c1[d1]) + a[d1]
            up = jnp.maximum(OPEN, c2[d2] - a[d2] + c3[u1]) + c2[u1] - a[u1]
            top = jnp.maximum(top, jnp.maximum(down, up))
        return top

    a = [clamp(d, lax.shift_right_arithmetic(c2[d] + c3[d] - c1[d] + 1, 1)) for d in range(4)]
    for d in range(4):
        b = [c2[e] - a[e] for e in range(4)]

        def down(s):
            return a[(s - 2) % 4] + c1[(s - 1) % 4] + a[(s - 1) % 4]

        def up(s):
            return b[(s + 2) % 4] + c3[(s + 1) % 4] + b[(s + 1) % 4]

        m = jnp.maximum(down((d + 2) % 4), down((d + 1) % 4)) - a[d]
        n = jnp.maximum(up((d + 2) % 4), up((d + 3) % 4)) - b[d]
        a[d] = clamp(d, lax.shift_right_arithmetic(n + c2[d] - m + 1, 1))
    top = worst(a)
    half = [lax.shift_right_logical(c2[d] + 1, 1) for d in range(4)]
    fits = top <= CAPACITY
    a = [jnp.where(fits, a[d], half[d]) for d in range(4)]
    top = jnp.where(fits, top, CAPACITY)
    b = [c2[d] - a[d] for d in range(4)]

    def at(values, index):
        index = lax.rem(index + 8, 4)
        out = values[3]
        for i in range(3):
            out = jnp.where(index == i, values[i], out)
        return out

    def entry(row, i):
        v = lists[row + i]
        return jnp.minimum(jnp.maximum(v, 0), CHIP - 1)

    d1, d2, u1 = lax.rem(chip + 3, 4), lax.rem(chip + 2, 4), lax.rem(chip + 1, 4)
    far_row = (d2 * 4 + 2) * 32
    a_far, b_far = at(a, d2), at(b, d2)
    down_fwd = jnp.maximum(OPEN, a_far + at(c1, d1))
    up_fwd = jnp.maximum(OPEN, b_far + at(c3, u1))
    for i in range(CAPACITY):
        plan_ref[i] = 0
        plan_ref[CAPACITY + i] = 0
    for i in range(FAR):
        plan_ref[i] = entry(far_row, i)
        plan_ref[CAPACITY + i] = entry(far_row, a_far + i)
    for i in range(PART):
        plan_ref[a_far + i] = entry((d1 * 4 + 1) * 32, i)
        plan_ref[CAPACITY + b_far + i] = entry((u1 * 4 + 3) * 32, i)
    for i in range(FAR):
        plan_ref[down_fwd + i] = CHIP + i
        plan_ref[CAPACITY + up_fwd + i] = CHIP + i

    own_a = at(a, chip)
    from_up = at(a, chip + 3)
    from_down = at(b, chip + 1)
    far_down = jnp.maximum(OPEN, at(a, chip + 3) + at(c1, chip))
    far_up = jnp.maximum(OPEN, at(b, chip + 1) + at(c3, chip))
    for j in range(PART):
        old = anc_ref[member * PART + j]
        src = third(old)
        k = lax.rem(src - chip + 4, 4)
        r = ranks[chip * 96 + old]
        far = jnp.where(r < own_a, CHIP + far_down + r, CHIP + CAPACITY + far_up + r - own_a)
        where = jnp.where(
            k == 0,
            old - src * CHIP,
            jnp.where(
                k == 1,
                CHIP + from_up + r,
                jnp.where(k == 3, CHIP + CAPACITY + from_down + r, far),
            ),
        )
        plan_ref[GATHER_AT + j] = where
    level = jnp.int32(0)
    for size in LEVELS[:-1]:
        level = level + jnp.where(top > size, 1, 0)
    plan_ref[LEVEL_AT] = level


def make_plan(ancestors):
    return pl.pallas_call(
        plan_kernel,
        out_shape=jax.ShapeDtypeStruct((64,), jnp.int32),
        in_specs=[pl.BlockSpec(memory_space=pltpu.SMEM)],
        out_specs=pl.BlockSpec(memory_space=pltpu.SMEM),
        scratch_shapes=[
            pltpu.SMEM((4 * 96,), jnp.int32),
            pltpu.SMEM((4 * 96,), jnp.int32),
            pltpu.SMEM((16 * 32,), jnp.int32),
        ],
    )(ancestors)


def one_step(u, v, h, cor, obs, nud, force):
    rows, lanes = u.shape
    row = lax.broadcasted_iota(jnp.int32, u.shape, 0)

    def across(q):
        return pltpu.roll(q, lanes - 1, 1) - pltpu.roll(q, 1, 1)

    def along(q):
        above = jnp.where(row == rows - 1, 0.0, pltpu.roll(q, rows - 1, 0))
        below = jnp.where(row == 0, 0.0, pltpu.roll(q, 1, 0))
        return above - below

    u_new = u + cor * v - 0.125 * across(h)
    v_new = v - cor * u - 0.125 * along(h)
    h_new = h - 0.125 * (across(u_new) + along(v_new)) + nud * (obs - h) + force
    return u_new, v_new, h_new


def cycle_kernel(
    size, plan, ens_hbm, pert_hbm, obs_hbm, prec_hbm, nud_hbm, cor_hbm,
    slots, lw_out,
    ens, pert, fields, cor_v, pool, first, stage, msg_out, msg_in, win, edge,
    misfit, zbuf, xbuf, lwbuf,
    in_sem, const_sem, halo_send, halo_recv, pool_send, pool_recv,
    ring_send, ring_recv, mir_send, mir_recv, out_sem,
    z_send, z_recv, x_send, x_recv, m_send, m_recv,
):
    member, lon = lax.axis_index("member"), lax.axis_index("lon")
    core = lax.rem(member, 2)
    lon_x, lon_z = lax.div(lon, 4), lax.rem(lon, 4)
    sibling = {"member": member + 1 - 2 * core}
    ring = ({"member": lax.rem(member + 6, 8)}, {"member": lax.rem(member + 2, 8)})
    sides = ({"lon": lax.rem(lon + 15, 16)}, {"lon": lax.rem(lon + 1, 16)})
    z_peers = [{"lon": lon_x * 4 + lax.rem(lon_z + k, 4)} for k in range(1, 4)]
    x_peers = [{"lon": lax.rem(lon_x + k, 4) * 4 + lon_z} for k in range(1, 4)]
    m_peers = [{"member": lax.rem(member + k, 8)} for k in range(1, 8)]

    def remote(src, dst, ssem, rsem, to):
        return pltpu.make_async_remote_copy(
            src_ref=src, dst_ref=dst, send_sem=ssem, recv_sem=rsem, device_id=to, device_id_type=MESH
        )

    loads = []
    for g in range(3):
        part = pl.ds(4 * g, 4)
        loads.append((
            pltpu.make_async_copy(ens_hbm.at[part], ens.at[part], in_sem.at[0, g]),
            pltpu.make_async_copy(pert_hbm.at[part], pert.at[part], in_sem.at[1, g]),
        ))
    consts = [
        pltpu.make_async_copy(ref, fields.at[i], const_sem.at[i])
        for i, ref in enumerate((obs_hbm, prec_hbm, nud_hbm))
    ] + [pltpu.make_async_copy(cor_hbm, cor_v, const_sem.at[3])]
    for cp in consts:
        cp.start()
    for pair in loads:
        for cp in pair:
            cp.start()

    barrier = pltpu.get_barrier_semaphore()
    everyone = list(sides) + z_peers + x_peers + m_peers
    for peer in everyone:
        pl.semaphore_signal(barrier, inc=1, device_id=peer, device_id_type=MESH)

    for cp in consts:
        cp.wait()
    for pair in loads:
        for cp in pair:
            cp.wait()

    lane = lax.broadcasted_iota(jnp.int32, (LAT, 128), 1)

    def tile(which, p, side):
        cut = slice(0, 128) if side == 0 else slice(128, 256)
        if which < 3:
            return ens[p, which, :, cut]
        if which < 6:
            return pert[p, which - 3, :, cut]
        return fields[0 if which == 6 else 2, :, cut]

    def turned(x, by):
        by = by % 128
        return x if by == 0 else pltpu.roll(x, by, 1)

    def item(which, p):
        i = which * PART + p if which < 5 else (60 if which == 6 else 61)
        return i // 21, 6 * (i % 21)

    items = [(f, p) for f in range(5) for p in range(PART)] + [(6, 0), (7, 0)]
    for side in range(2):
        start = 0 if side == 0 else 122
        acc = [None] * 3
        for f, p in items:
            t, o = item(f, p)
            x = turned(tile(f, p, side), o - start)
            acc[t] = x if acc[t] is None else jnp.where(lane >= o, x, acc[t])
        for t in range(3):
            msg_out[side, t] = acc[t]

    pl.semaphore_wait(barrier, len(everyone))
    halos = [
        remote(msg_out.at[s], msg_in.at[1 - s], halo_send.at[s], halo_recv.at[1 - s], sides[s])
        for s in range(2)
    ]
    for cp in halos:
        cp.start()

    def interior(p, carry):
        cor = jnp.concatenate([cor_v[...], cor_v[...]], axis=1)
        u, v, h = ens[p, 0], ens[p, 1], ens[p, 2]
        for step in range(STEPS):
            u, v, h = one_step(u, v, h, cor, fields[0], fields[2], pert[p, step])
        at = core * PART + p
        pool[at, 0], pool[at, 1], pool[at, 2] = u, v, h
        return carry

    lax.fori_loop(0, PART, interior, 0)

    for s in range(2):
        remote(msg_out.at[s], msg_in.at[s], halo_send.at[s], halo_recv.at[s], sides[s]).wait_recv()
    for s in range(2):
        for half in range(2):
            members = list(range(half * PER_TILE, min(PART, (half + 1) * PER_TILE)))
            for f in range(8):
                if f >= 6 and half == 1:
                    continue
                count = PER_TILE if f >= 6 else len(members)
                acc = None
                for q in range(count):
                    p = members[q] if f < 6 else 0
                    o = WIN * q
                    if s == 0:
                        own, own_o = turned(tile(f, p, 0), o + HALO), o + HALO
                        nb_o = o
                    else:
                        own, own_o = turned(tile(f, p, 1), o - 116), o
                        nb_o = o + 2 * HALO
                    parts = [(own_o, own)]
                    if f != 5:
                        t, io = item(f, p)
                        nb = turned(msg_in[s, t], nb_o - io)
                        parts.append((nb_o, nb))
                    parts.sort(key=lambda e: e[0])
                    for off, x in parts:
                        acc = x if acc is None else jnp.where(lane >= off, x, acc)
                win[s, half, f] = acc
    for s in range(2):
        for half in range(2):
            u, v, h = win[s, half, 0], win[s, half, 1], win[s, half, 2]
            for step in range(STEPS):
                u, v, h = one_step(u, v, h, cor_v[...], win[s, 0, 6], win[s, 0, 7], win[s, half, 3 + step])
            edge[s, half, 0], edge[s, half, 1], edge[s, half, 2] = u, v, h

    shares = []
    for p in range(PART):
        at = core * PART + p
        half, q = p // PER_TILE, p % PER_TILE
        for f in range(3):
            left = turned(edge[0, half, f], -(WIN * q + HALO))
            right = turned(edge[1, half, f], 122 - (WIN * q + HALO))
            low = jnp.where(lane < HALO, left, pool[at, f, :, 0:128])
            high = jnp.where(lane >= 122, right, pool[at, f, :, 128:256])
            pool[at, f, :, 0:128] = low
            pool[at, f, :, 128:256] = high
        cp = remote(pool.at[at], pool.at[at], pool_send.at[p], pool_recv.at[p], sibling)
        cp.start()
        shares.append(cp)
        lo = fields[0, :, 0:128] - low
        hi = fields[0, :, 128:256] - high
        term = fields[1, :, 0:128] * lo * lo + fields[1, :, 128:256] * hi * hi
        misfit[p:p + 1, :] = jnp.sum(term, axis=0, keepdims=True)

    total = jnp.sum(misfit[...], axis=1, keepdims=True)
    small = lax.broadcasted_iota(jnp.int32, (PART, 128), 1)
    which = lax.broadcasted_iota(jnp.int32, (PART, 128), 0)
    line = jnp.sum(jnp.where(small == which, total, 0.0), axis=0, keepdims=True)
    zbuf[lon_z] = jnp.broadcast_to(line, (8, 128))
    z_copies = [
        remote(zbuf.at[lon_z], zbuf.at[lon_z], z_send.at[k], z_recv.at[k], z_peers[k]) for k in range(3)
    ]
    for cp in z_copies:
        cp.start()

    for p in range(PART):
        other = (1 - core) * PART + p
        remote(pool.at[other], pool.at[other], pool_send.at[p], pool_recv.at[p], sibling).wait_recv()
    keep = [pltpu.make_async_copy(pool, slots.at[pl.ds(0, CHIP)], out_sem.at[0])]
    keep[0].start()

    lanes_per_core = size // 2
    open_pos, far_pos = OPEN // 2, FAR // 2

    def landing(way, pos, on_core):
        i = 2 * pos + on_core
        if pos < far_pos:
            return first.at[way, i]
        return slots.at[CHIP + way * CAPACITY + i]

    def ring_copy(way, pos):
        return remote(
            stage.at[way, pos], landing(way, pos, core), ring_send.at[way, pos], ring_recv.at[way, pos], ring[way]
        )

    def mirror_copy(way, pos, on_core):
        ref = landing(way, pos, on_core)
        return remote(ref, ref, mir_send.at[way, pos], mir_recv.at[way, pos], sibling)

    for pos in range(open_pos):
        for way in range(2):
            stage[way, pos] = pool[plan[way * CAPACITY + 2 * pos + core]]
            ring_copy(way, pos).start()

    for k in range(3):
        z_copies[k].wait_send()
        z_copies[k].wait_recv()
    xbuf[lon_x] = ((zbuf[0] + zbuf[1]) + zbuf[2]) + zbuf[3]
    x_copies = [
        remote(xbuf.at[lon_x], xbuf.at[lon_x], x_send.at[k], x_recv.at[k], x_peers[k]) for k in range(3)
    ]
    for cp in x_copies:
        cp.start()
    for cp in x_copies:
        cp.wait_send()
        cp.wait_recv()
    lwbuf[member] = ((xbuf[0] + xbuf[1]) + xbuf[2]) + xbuf[3]
    m_copies = [
        remote(lwbuf.at[member], lwbuf.at[member], m_send.at[k], m_recv.at[k], m_peers[k]) for k in range(7)
    ]
    for cp in m_copies:
        cp.start()

    for pos in range(far_pos):
        for way in range(2):
            ring_copy(way, pos).wait_recv()
            mirror_copy(way, pos, core).start()
    for pos in range(far_pos):
        for way in range(2):
            mirror_copy(way, pos, 1 - core).wait_recv()
    for way in range(2):
        cp = pltpu.make_async_copy(
            first.at[way], slots.at[pl.ds(CHIP + way * CAPACITY, FAR)], out_sem.at[1 + way]
        )
        cp.start()
        keep.append(cp)
    for pos in range(open_pos, lanes_per_core):
        for way in range(2):
            idx = plan[way * CAPACITY + 2 * pos + core]
            own = pool[jnp.minimum(idx, CHIP - 1)]
            passed = first[way, jnp.clip(idx - CHIP, 0, FAR - 1)]
            stage[way, pos] = jnp.where(idx < CHIP, own, passed)
            ring_copy(way, pos).start()
    for pos in range(far_pos, lanes_per_core):
        for way in range(2):
            ring_copy(way, pos).wait_recv()
            mirror_copy(way, pos, core).start()

    for cp in m_copies:
        cp.wait_send()
        cp.wait_recv()
    lw_out[...] = lwbuf[...]
    for cp in halos + shares:
        cp.wait_send()
    for pos in range(lanes_per_core):
        for way in range(2):
            ring_copy(way, pos).wait_send()
    for pos in range(lanes_per_core):
        for way in range(2):
            mirror_copy(way, pos, core).wait_send()
            if pos >= far_pos:
                mirror_copy(way, pos, 1 - core).wait_recv()
    for cp in keep:
        cp.wait()


def run_cycle(size, number, plan, ensemble, perturbation, observed, precision, nudging, coriolis):
    anywhere = pl.BlockSpec(memory_space=pl.ANY)
    dma = pltpu.SemaphoreType.DMA
    most = size // 2
    return pl.pallas_call(
        functools.partial(cycle_kernel, size),
        out_shape=(
            jax.ShapeDtypeStruct((SLOTS, 3, LAT, CLON), F32),
            jax.ShapeDtypeStruct((8, 8, 128), F32),
        ),
        in_specs=[pl.BlockSpec(memory_space=pltpu.SMEM)] + [anywhere] * 6,
        out_specs=(anywhere, pl.BlockSpec(memory_space=pltpu.VMEM)),
        scratch_shapes=[
            pltpu.VMEM((PART, 3, LAT, CLON), F32),
            pltpu.VMEM((PART, 3, LAT, CLON), F32),
            pltpu.VMEM((3, LAT, CLON), F32),
            pltpu.VMEM((LAT, 128), F32),
            pltpu.VMEM((CHIP, 3, LAT, CLON), F32),
            pltpu.VMEM((2, FAR, 3, LAT, CLON), F32),
            pltpu.VMEM((2, most, 3, LAT, CLON), F32),
            pltpu.VMEM((2, 3, LAT, 128), F32),
            pltpu.VMEM((2, 3, LAT, 128), F32),
            pltpu.VMEM((2, 2, 8, LAT, 128), F32),
            pltpu.VMEM((2, 2, 3, LAT, 128), F32),
            pltpu.VMEM((PART, 128), F32),
            pltpu.VMEM((4, 8, 128), F32),
            pltpu.VMEM((4, 8, 128), F32),
            pltpu.VMEM((8, 8, 128), F32),
            dma((2, 3)), dma((4,)), dma((2,)), dma((2,)), dma((PART,)), dma((PART,)),
            dma((2, most)), dma((2, most)), dma((2, most)), dma((2, most)), dma((3,)),
            dma((3,)), dma((3,)), dma((3,)), dma((3,)), dma((7,)), dma((7,)),
        ],
        compiler_params=pltpu.CompilerParams(
            collective_id=number, has_side_effects=True, vmem_limit_bytes=50 * 2**20
        ),
    )(plan, ensemble, perturbation, observed, precision, nudging, coriolis)


def resample_kernel(plan, lw_ref, slots, weights_ref, analysis, sems):
    copies = [
        pltpu.make_async_copy(slots.at[plan[GATHER_AT + j]], analysis.at[j], sems.at[j]) for j in range(PART)
    ]
    for cp in copies:
        cp.start()
    lane = lax.broadcasted_iota(jnp.int32, (8, 8, 128), 2)
    logw = jnp.where(lane < PART, lw_ref[...] * (-2.0 / (LAT * CLON * 16)), -jnp.inf)
    top = jnp.max(jnp.max(logw, axis=0), axis=1, keepdims=True)
    e = jnp.exp(logw - top[None])
    whole = jnp.sum(jnp.sum(e, axis=0), axis=1, keepdims=True)
    own = jnp.where(
        lax.broadcasted_iota(jnp.int32, (8, 8, 128), 0) == lax.axis_index("member"), e, 0.0
    )
    row = jnp.sum(own, axis=0) / whole
    weights_ref[...] = row[0, :PART]
    for cp in copies:
        cp.wait()


def resample(plan, lw, slots):
    return pl.pallas_call(
        resample_kernel,
        out_shape=(
            jax.ShapeDtypeStruct((PART,), F32),
            jax.ShapeDtypeStruct((PART, 3, LAT, CLON), F32),
        ),
        in_specs=[
            pl.BlockSpec(memory_space=pltpu.SMEM),
            pl.BlockSpec(memory_space=pltpu.VMEM),
            pl.BlockSpec(memory_space=pl.ANY),
        ],
        out_specs=(pl.BlockSpec(memory_space=pltpu.VMEM), pl.BlockSpec(memory_space=pl.ANY)),
        scratch_shapes=[pltpu.SemaphoreType.DMA((PART,))],
    )(plan, lw, slots)


def body(ensemble, perturbation, observed, precision, nudging, ancestors):
    rows = np.arange(LAT).astype(np.float32)
    cor = (0.3 * np.sin(np.float32(math.pi) * (rows + np.float32(0.5 - LAT / 2)) / np.float32(LAT))).astype(np.float32)
    coriolis = jnp.asarray(np.broadcast_to(cor[:, None], (LAT, 128)))
    plan = make_plan(ancestors)
    operands = (plan, ensemble, perturbation, observed, precision, nudging, coriolis)
    branches = [functools.partial(run_cycle, size, n) for n, size in enumerate(LEVELS)]
    if len(branches) == 1:
        slots, lw = branches[0](*operands)
    else:
        slots, lw = lax.switch(plan[LEVEL_AT], branches, *operands)
    weights, analysis = resample(plan, lw, slots)
    return weights, analysis


def solution(mesh):
    placed = (
        P("member", None, None, "lon"),
        P("member", None, None, "lon"),
        P(None, "lon"),
        P(None, "lon"),
        P(None, "lon"),
        P(),
    )
    return jax.shard_map(
        body,
        mesh=mesh,
        in_specs=placed,
        out_specs=(P("member"), P("member", None, None, "lon")),
        check_vma=False,
    )
```

```python
import functools
import math

import jax
import jax.numpy as jnp
from jax import lax
from jax.experimental import pallas as pl
from jax.experimental.pallas import tpu as pltpu
from jax.sharding import PartitionSpec as P

MESH = pl.DeviceIdType.MESH
F32 = jnp.float32
STEPS = 3
LAT = 64
CLON = 256
PART = 12
CHIP = 24
HALO = 6
WIN = 18
PER_TILE = 7
FAR = 6
OPEN = 8
CAPACITY = 24
LEVELS = (12, 14, 24)
SLOTS = CHIP + 2 * CAPACITY
GATHER_AT = 2 * CAPACITY
LEVEL_AT = GATHER_AT + PART


def plan_kernel(anc_ref, plan_ref, need, ranks, lists):
    member = lax.axis_index("member")
    chip = lax.div(member, 2)

    def third(a):
        return lax.shift_right_logical(a * 2731, 16)

    for i in range(4 * 96):
        need[i] = 0
    for j in range(96):
        need[(j // CHIP) * 96 + anc_ref[j]] = 1
    counts = {}
    for d in range(4):
        for k in range(1, 4):
            s = (d + k) % 4
            cnt = jnp.int32(0)
            for p in range(CHIP):
                v = need[d * 96 + s * CHIP + p]
                ranks[d * 96 + s * CHIP + p] = cnt
                lists[(d * 4 + k) * 32 + cnt] = p
                cnt = cnt + v
            counts[d, k] = cnt
    c1 = [counts[d, 1] for d in range(4)]
    c2 = [counts[d, 2] for d in range(4)]
    c3 = [counts[d, 3] for d in range(4)]

    def clamp(d, x):
        return jnp.minimum(jnp.maximum(x, jnp.maximum(0, c2[d] - FAR)), jnp.minimum(FAR, c2[d]))

    def worst(a):
        top = jnp.int32(0)
        for s in range(4):
            d1, d2, u1 = (s - 1) % 4, (s - 2) % 4, (s + 1) % 4
            down = jnp.maximum(OPEN, a[d2] + c1[d1]) + a[d1]
            up = jnp.maximum(OPEN, c2[d2] - a[d2] + c3[u1]) + c2[u1] - a[u1]
            top = jnp.maximum(top, jnp.maximum(down, up))
        return top

    a = [clamp(d, lax.shift_right_arithmetic(c2[d] + c3[d] - c1[d] + 1, 1)) for d in range(4)]
    for d in range(4):
        b = [c2[e] - a[e] for e in range(4)]

        def down(s):
            return a[(s - 2) % 4] + c1[(s - 1) % 4] + a[(s - 1) % 4]

        def up(s):
            return b[(s + 2) % 4] + c3[(s + 1) % 4] + b[(s + 1) % 4]

        m = jnp.maximum(down((d + 2) % 4), down((d + 1) % 4)) - a[d]
        n = jnp.maximum(up((d + 2) % 4), up((d + 3) % 4)) - b[d]
        a[d] = clamp(d, lax.shift_right_arithmetic(n + c2[d] - m + 1, 1))
    top = worst(a)
    half = [lax.shift_right_logical(c2[d] + 1, 1) for d in range(4)]
    fits = top <= CAPACITY
    a = [jnp.where(fits, a[d], half[d]) for d in range(4)]
    top = jnp.where(fits, top, CAPACITY)
    b = [c2[d] - a[d] for d in range(4)]

    def at(values, index):
        index = lax.rem(index + 8, 4)
        out = values[3]
        for i in range(3):
            out = jnp.where(index == i, values[i], out)
        return out

    def entry(row, i):
        v = lists[row + i]
        return jnp.minimum(jnp.maximum(v, 0), CHIP - 1)

    d1, d2, u1 = lax.rem(chip + 3, 4), lax.rem(chip + 2, 4), lax.rem(chip + 1, 4)
    far_row = (d2 * 4 + 2) * 32
    a_far, b_far = at(a, d2), at(b, d2)
    down_fwd = jnp.maximum(OPEN, a_far + at(c1, d1))
    up_fwd = jnp.maximum(OPEN, b_far + at(c3, u1))
    for i in range(CAPACITY):
        plan_ref[i] = 0
        plan_ref[CAPACITY + i] = 0
    for i in range(FAR):
        plan_ref[i] = entry(far_row, i)
        plan_ref[CAPACITY + i] = entry(far_row, a_far + i)
    for i in range(PART):
        plan_ref[a_far + i] = entry((d1 * 4 + 1) * 32, i)
        plan_ref[CAPACITY + b_far + i] = entry((u1 * 4 + 3) * 32, i)
    for i in range(FAR):
        plan_ref[down_fwd + i] = CHIP + i
        plan_ref[CAPACITY + up_fwd + i] = CHIP + i

    own_a = at(a, chip)
    from_up = at(a, chip + 3)
    from_down = at(b, chip + 1)
    far_down = jnp.maximum(OPEN, at(a, chip + 3) + at(c1, chip))
    far_up = jnp.maximum(OPEN, at(b, chip + 1) + at(c3, chip))
    for j in range(PART):
        old = anc_ref[member * PART + j]
        src = third(old)
        k = lax.rem(src - chip + 4, 4)
        r = ranks[chip * 96 + old]
        far = jnp.where(r < own_a, CHIP + far_down + r, CHIP + CAPACITY + far_up + r - own_a)
        where = jnp.where(
            k == 0,
            old - src * CHIP,
            jnp.where(
                k == 1,
                CHIP + from_up + r,
                jnp.where(k == 3, CHIP + CAPACITY + from_down + r, far),
            ),
        )
        plan_ref[GATHER_AT + j] = where
    level = jnp.int32(0)
    for size in LEVELS[:-1]:
        level = level + jnp.where(top > size, 1, 0)
    plan_ref[LEVEL_AT] = level


def make_plan(ancestors):
    return pl.pallas_call(
        plan_kernel,
        out_shape=jax.ShapeDtypeStruct((64,), jnp.int32),
        in_specs=[pl.BlockSpec(memory_space=pltpu.SMEM)],
        out_specs=pl.BlockSpec(memory_space=pltpu.SMEM),
        scratch_shapes=[
            pltpu.SMEM((4 * 96,), jnp.int32),
            pltpu.SMEM((4 * 96,), jnp.int32),
            pltpu.SMEM((16 * 32,), jnp.int32),
        ],
    )(ancestors)


def one_step(u, v, h, cor, obs, nud, force):
    rows, lanes = u.shape
    row = lax.broadcasted_iota(jnp.int32, u.shape, 0)

    def across(q):
        return pltpu.roll(q, lanes - 1, 1) - pltpu.roll(q, 1, 1)

    def along(q):
        above = jnp.where(row == rows - 1, 0.0, pltpu.roll(q, rows - 1, 0))
        below = jnp.where(row == 0, 0.0, pltpu.roll(q, 1, 0))
        return above - below

    u_new = u + cor * v - 0.125 * across(h)
    v_new = v - cor * u - 0.125 * along(h)
    h_new = h - 0.125 * (across(u_new) + along(v_new)) + nud * (obs - h) + force
    return u_new, v_new, h_new


def cycle_kernel(
    size, plan, ens_hbm, pert_hbm, obs_hbm, prec_hbm, nud_hbm,
    slots, lw_out,
    ens, pert, fields, cor_v, pool, first, stage, msg_out, msg_in, win, edge,
    misfit, zbuf, xbuf, lwbuf,
    in_sem, const_sem, halo_send, halo_recv, pool_send, pool_recv,
    ring_send, ring_recv, mir_send, mir_recv, out_sem,
    z_send, z_recv, x_send, x_recv, m_send, m_recv,
):
    member, lon = lax.axis_index("member"), lax.axis_index("lon")
    core = lax.rem(member, 2)
    lon_x, lon_z = lax.div(lon, 4), lax.rem(lon, 4)
    sibling = {"member": member + 1 - 2 * core}
    ring = ({"member": lax.rem(member + 6, 8)}, {"member": lax.rem(member + 2, 8)})
    sides = ({"lon": lax.rem(lon + 15, 16)}, {"lon": lax.rem(lon + 1, 16)})
    z_peers = [{"lon": lon_x * 4 + lax.rem(lon_z + k, 4)} for k in range(1, 4)]
    x_peers = [{"lon": lax.rem(lon_x + k, 4) * 4 + lon_z} for k in range(1, 4)]
    m_peers = [{"member": lax.rem(member + k, 8)} for k in range(1, 8)]

    def remote(src, dst, ssem, rsem, to):
        return pltpu.make_async_remote_copy(
            src_ref=src, dst_ref=dst, send_sem=ssem, recv_sem=rsem, device_id=to, device_id_type=MESH
        )

    loads = []
    for g in range(3):
        part = pl.ds(4 * g, 4)
        loads.append((
            pltpu.make_async_copy(ens_hbm.at[part], ens.at[part], in_sem.at[0, g]),
            pltpu.make_async_copy(pert_hbm.at[part], pert.at[part], in_sem.at[1, g]),
        ))
    consts = [
        pltpu.make_async_copy(ref, fields.at[i], const_sem.at[i])
        for i, ref in enumerate((obs_hbm, prec_hbm, nud_hbm))
    ]
    for cp in consts:
        cp.start()
    for pair in loads:
        for cp in pair:
            cp.start()

    barrier = pltpu.get_barrier_semaphore()
    everyone = list(sides) + z_peers + x_peers + m_peers
    for peer in everyone:
        pl.semaphore_signal(barrier, inc=1, device_id=peer, device_id_type=MESH)

    row_at = lax.broadcasted_iota(jnp.int32, (LAT, 128), 0).astype(F32)
    cor_v[...] = 0.3 * jnp.sin(math.pi * (row_at + 0.5 - LAT / 2) / LAT)

    for cp in consts:
        cp.wait()
    for pair in loads:
        for cp in pair:
            cp.wait()

    lane = lax.broadcasted_iota(jnp.int32, (LAT, 128), 1)

    def tile(which, p, side):
        cut = slice(0, 128) if side == 0 else slice(128, 256)
        if which < 3:
            return ens[p, which, :, cut]
        if which < 6:
            return pert[p, which - 3, :, cut]
        return fields[0 if which == 6 else 2, :, cut]

    def turned(x, by):
        by = by % 128
        return x if by == 0 else pltpu.roll(x, by, 1)

    def item(which, p):
        i = which * PART + p if which < 5 else (60 if which == 6 else 61)
        return i // 21, 6 * (i % 21)

    items = [(f, p) for f in range(5) for p in range(PART)] + [(6, 0), (7, 0)]
    for side in range(2):
        start = 0 if side == 0 else 122
        acc = [None] * 3
        for f, p in items:
            t, o = item(f, p)
            x = turned(tile(f, p, side), o - start)
            acc[t] = x if acc[t] is None else jnp.where(lane >= o, x, acc[t])
        for t in range(3):
            msg_out[side, t] = acc[t]

    pl.semaphore_wait(barrier, len(everyone))
    halos = [
        remote(msg_out.at[s], msg_in.at[1 - s], halo_send.at[s], halo_recv.at[1 - s], sides[s])
        for s in range(2)
    ]
    for cp in halos:
        cp.start()

    def interior(p, carry):
        cor = jnp.concatenate([cor_v[...], cor_v[...]], axis=1)
        u, v, h = ens[p, 0], ens[p, 1], ens[p, 2]
        for step in range(STEPS):
            u, v, h = one_step(u, v, h, cor, fields[0], fields[2], pert[p, step])
        at = core * PART + p
        pool[at, 0], pool[at, 1], pool[at, 2] = u, v, h
        return carry

    lax.fori_loop(0, PART, interior, 0)

    for s in range(2):
        remote(msg_out.at[s], msg_in.at[s], halo_send.at[s], halo_recv.at[s], sides[s]).wait_recv()
    for s in range(2):
        for half in range(2):
            members = list(range(half * PER_TILE, min(PART, (half + 1) * PER_TILE)))
            for f in range(8):
                if f >= 6 and half == 1:
                    continue
                count = PER_TILE if f >= 6 else len(members)
                acc = None
                for q in range(count):
                    p = members[q] if f < 6 else 0
                    o = WIN * q
                    if s == 0:
                        own, own_o = turned(tile(f, p, 0), o + HALO), o + HALO
                        nb_o = o
                    else:
                        own, own_o = turned(tile(f, p, 1), o - 116), o
                        nb_o = o + 2 * HALO
                    parts = [(own_o, own)]
                    if f != 5:
                        t, io = item(f, p)
                        nb = turned(msg_in[s, t], nb_o - io)
                        parts.append((nb_o, nb))
                    parts.sort(key=lambda e: e[0])
                    for off, x in parts:
                        acc = x if acc is None else jnp.where(lane >= off, x, acc)
                win[s, half, f] = acc
    for s in range(2):
        for half in range(2):
            u, v, h = win[s, half, 0], win[s, half, 1], win[s, half, 2]
            for step in range(STEPS):
                u, v, h = one_step(u, v, h, cor_v[...], win[s, 0, 6], win[s, 0, 7], win[s, half, 3 + step])
            edge[s, half, 0], edge[s, half, 1], edge[s, half, 2] = u, v, h

    shares = []
    for p in range(PART):
        at = core * PART + p
        half, q = p // PER_TILE, p % PER_TILE
        for f in range(3):
            left = turned(edge[0, half, f], -(WIN * q + HALO))
            right = turned(edge[1, half, f], 122 - (WIN * q + HALO))
            low = jnp.where(lane < HALO, left, pool[at, f, :, 0:128])
            high = jnp.where(lane >= 122, right, pool[at, f, :, 128:256])
            pool[at, f, :, 0:128] = low
            pool[at, f, :, 128:256] = high
        cp = remote(pool.at[at], pool.at[at], pool_send.at[p], pool_recv.at[p], sibling)
        cp.start()
        shares.append(cp)
        lo = fields[0, :, 0:128] - low
        hi = fields[0, :, 128:256] - high
        term = fields[1, :, 0:128] * lo * lo + fields[1, :, 128:256] * hi * hi
        misfit[p:p + 1, :] = jnp.sum(term, axis=0, keepdims=True)

    total = jnp.sum(misfit[...], axis=1, keepdims=True)
    small = lax.broadcasted_iota(jnp.int32, (PART, 128), 1)
    which = lax.broadcasted_iota(jnp.int32, (PART, 128), 0)
    line = jnp.sum(jnp.where(small == which, total, 0.0), axis=0, keepdims=True)
    zbuf[lon_z] = jnp.broadcast_to(line, (8, 128))
    z_copies = [
        remote(zbuf.at[lon_z], zbuf.at[lon_z], z_send.at[k], z_recv.at[k], z_peers[k]) for k in range(3)
    ]
    for cp in z_copies:
        cp.start()

    for p in range(PART):
        other = (1 - core) * PART + p
        remote(pool.at[other], pool.at[other], pool_send.at[p], pool_recv.at[p], sibling).wait_recv()
    keep = [pltpu.make_async_copy(pool, slots.at[pl.ds(0, CHIP)], out_sem.at[0])]
    keep[0].start()

    lanes_per_core = size // 2
    open_pos, far_pos = OPEN // 2, FAR // 2

    def landing(way, pos, on_core):
        i = 2 * pos + on_core
        if pos < far_pos:
            return first.at[way, i]
        return slots.at[CHIP + way * CAPACITY + i]

    def ring_copy(way, pos):
        return remote(
            stage.at[way, pos], landing(way, pos, core), ring_send.at[way, pos], ring_recv.at[way, pos], ring[way]
        )

    def mirror_copy(way, pos, on_core):
        ref = landing(way, pos, on_core)
        return remote(ref, ref, mir_send.at[way, pos], mir_recv.at[way, pos], sibling)

    for pos in range(open_pos):
        for way in range(2):
            stage[way, pos] = pool[plan[way * CAPACITY + 2 * pos + core]]
            ring_copy(way, pos).start()

    for k in range(3):
        z_copies[k].wait_send()
        z_copies[k].wait_recv()
    xbuf[lon_x] = ((zbuf[0] + zbuf[1]) + zbuf[2]) + zbuf[3]
    x_copies = [
        remote(xbuf.at[lon_x], xbuf.at[lon_x], x_send.at[k], x_recv.at[k], x_peers[k]) for k in range(3)
    ]
    for cp in x_copies:
        cp.start()
    for cp in x_copies:
        cp.wait_send()
        cp.wait_recv()
    lwbuf[member] = ((xbuf[0] + xbuf[1]) + xbuf[2]) + xbuf[3]
    m_copies = [
        remote(lwbuf.at[member], lwbuf.at[member], m_send.at[k], m_recv.at[k], m_peers[k]) for k in range(7)
    ]
    for cp in m_copies:
        cp.start()

    for pos in range(far_pos):
        for way in range(2):
            ring_copy(way, pos).wait_recv()
            mirror_copy(way, pos, core).start()
    for pos in range(far_pos):
        for way in range(2):
            mirror_copy(way, pos, 1 - core).wait_recv()
    for way in range(2):
        cp = pltpu.make_async_copy(
            first.at[way], slots.at[pl.ds(CHIP + way * CAPACITY, FAR)], out_sem.at[1 + way]
        )
        cp.start()
        keep.append(cp)
    for pos in range(open_pos, lanes_per_core):
        for way in range(2):
            idx = plan[way * CAPACITY + 2 * pos + core]
            own = pool[jnp.minimum(idx, CHIP - 1)]
            passed = first[way, jnp.clip(idx - CHIP, 0, FAR - 1)]
            stage[way, pos] = jnp.where(idx < CHIP, own, passed)
            ring_copy(way, pos).start()
    for pos in range(far_pos, lanes_per_core):
        for way in range(2):
            ring_copy(way, pos).wait_recv()
            mirror_copy(way, pos, core).start()

    for cp in m_copies:
        cp.wait_send()
        cp.wait_recv()
    lw_out[...] = lwbuf[...]
    for cp in halos + shares:
        cp.wait_send()
    for pos in range(lanes_per_core):
        for way in range(2):
            ring_copy(way, pos).wait_send()
    for pos in range(lanes_per_core):
        for way in range(2):
            mirror_copy(way, pos, core).wait_send()
            if pos >= far_pos:
                mirror_copy(way, pos, 1 - core).wait_recv()
    for cp in keep:
        cp.wait()


def run_cycle(size, number, plan, ensemble, perturbation, observed, precision, nudging):
    anywhere = pl.BlockSpec(memory_space=pltpu.HBM)
    dma = pltpu.SemaphoreType.DMA
    most = size // 2
    return pl.pallas_call(
        functools.partial(cycle_kernel, size),
        out_shape=(
            jax.ShapeDtypeStruct((SLOTS, 3, LAT, CLON), F32),
            jax.ShapeDtypeStruct((8, 8, 128), F32),
        ),
        in_specs=[pl.BlockSpec(memory_space=pltpu.SMEM)] + [anywhere] * 5,
        out_specs=(anywhere, pl.BlockSpec(memory_space=pltpu.VMEM)),
        scratch_shapes=[
            pltpu.VMEM((PART, 3, LAT, CLON), F32),
            pltpu.VMEM((PART, 3, LAT, CLON), F32),
            pltpu.VMEM((3, LAT, CLON), F32),
            pltpu.VMEM((LAT, 128), F32),
            pltpu.VMEM((CHIP, 3, LAT, CLON), F32),
            pltpu.VMEM((2, FAR, 3, LAT, CLON), F32),
            pltpu.VMEM((2, most, 3, LAT, CLON), F32),
            pltpu.VMEM((2, 3, LAT, 128), F32),
            pltpu.VMEM((2, 3, LAT, 128), F32),
            pltpu.VMEM((2, 2, 8, LAT, 128), F32),
            pltpu.VMEM((2, 2, 3, LAT, 128), F32),
            pltpu.VMEM((PART, 128), F32),
            pltpu.VMEM((4, 8, 128), F32),
            pltpu.VMEM((4, 8, 128), F32),
            pltpu.VMEM((8, 8, 128), F32),
            dma((2, 3)), dma((3,)), dma((2,)), dma((2,)), dma((PART,)), dma((PART,)),
            dma((2, most)), dma((2, most)), dma((2, most)), dma((2, most)), dma((3,)),
            dma((3,)), dma((3,)), dma((3,)), dma((3,)), dma((7,)), dma((7,)),
        ],
        compiler_params=pltpu.CompilerParams(
            collective_id=number, has_side_effects=True, vmem_limit_bytes=50 * 2**20
        ),
    )(plan, ensemble, perturbation, observed, precision, nudging)


def resample_kernel(plan, lw_ref, slots, weights_ref, analysis, held, in_sem, out_sem):
    ins = [
        pltpu.make_async_copy(slots.at[plan[GATHER_AT + j]], held.at[j], in_sem.at[j]) for j in range(PART)
    ]
    outs = [pltpu.make_async_copy(held.at[j], analysis.at[j], out_sem.at[j]) for j in range(PART)]
    for cp in ins:
        cp.start()
    lane = lax.broadcasted_iota(jnp.int32, (8, 8, 128), 2)
    logw = jnp.where(lane < PART, lw_ref[...] * (-2.0 / (LAT * CLON * 16)), -jnp.inf)
    top = jnp.max(jnp.max(logw, axis=0), axis=1, keepdims=True)
    e = jnp.exp(logw - top[None])
    whole = jnp.sum(jnp.sum(e, axis=0), axis=1, keepdims=True)
    own = jnp.where(
        lax.broadcasted_iota(jnp.int32, (8, 8, 128), 0) == lax.axis_index("member"), e, 0.0
    )
    row = jnp.sum(own, axis=0) / whole
    weights_ref[...] = row[0, :PART]
    for j in range(PART):
        ins[j].wait()
        outs[j].start()
    for cp in outs:
        cp.wait()


def resample(plan, lw, slots):
    return pl.pallas_call(
        resample_kernel,
        out_shape=(
            jax.ShapeDtypeStruct((PART,), F32),
            jax.ShapeDtypeStruct((PART, 3, LAT, CLON), F32),
        ),
        in_specs=[
            pl.BlockSpec(memory_space=pltpu.SMEM),
            pl.BlockSpec(memory_space=pltpu.VMEM),
            pl.BlockSpec(memory_space=pltpu.HBM),
        ],
        out_specs=(pl.BlockSpec(memory_space=pltpu.VMEM), pl.BlockSpec(memory_space=pltpu.HBM)),
        scratch_shapes=[
            pltpu.VMEM((PART, 3, LAT, CLON), F32),
            pltpu.SemaphoreType.DMA((PART,)),
            pltpu.SemaphoreType.DMA((PART,)),
        ],
    )(plan, lw, slots)


def body(ensemble, perturbation, observed, precision, nudging, ancestors):
    plan = make_plan(ancestors)
    operands = (plan, ensemble, perturbation, observed, precision, nudging)
    branches = [functools.partial(run_cycle, size, n) for n, size in enumerate(LEVELS)]
    if len(branches) == 1:
        slots, lw = branches[0](*operands)
    else:
        slots, lw = lax.switch(plan[LEVEL_AT], branches, *operands)
    weights, analysis = resample(plan, lw, slots)
    return weights, analysis


def solution(mesh):
    placed = (
        P("member", None, None, "lon"),
        P("member", None, None, "lon"),
        P(None, "lon"),
        P(None, "lon"),
        P(None, "lon"),
        P(),
    )
    return jax.shard_map(
        body,
        mesh=mesh,
        in_specs=placed,
        out_specs=(P("member"), P("member", None, None, "lon")),
        check_vma=False,
    )
```

```python
import functools
import math

import jax
import jax.numpy as jnp
from jax import lax
from jax.experimental import pallas as pl
from jax.experimental.pallas import tpu as pltpu
from jax.sharding import PartitionSpec as P

MESH = pl.DeviceIdType.MESH
F32 = jnp.float32
STEPS = 3
LAT = 64
CLON = 256
PART = 12
CHIP = 24
HALO = 6
WIN = 18
PER_TILE = 7
FAR = 6
OPEN = 8
CAPACITY = 24
LEVELS = (12, 13, 14, 16, 24)
SLOTS = CHIP + 2 * CAPACITY
GATHER_AT = 2 * CAPACITY


def plan_kernel(anc_ref, plan_ref, level_ref, need, ranks, lists):
    member = lax.axis_index("member")
    chip = lax.div(member, 2)

    def third(a):
        return lax.shift_right_logical(a * 2731, 16)

    for i in range(4 * 96):
        need[i] = 0
    for j in range(96):
        need[(j // CHIP) * 96 + anc_ref[j]] = 1
    counts = {}
    for d in range(4):
        for k in range(1, 4):
            s = (d + k) % 4
            cnt = jnp.int32(0)
            for p in range(CHIP):
                v = need[d * 96 + s * CHIP + p]
                ranks[d * 96 + s * CHIP + p] = cnt
                lists[(d * 4 + k) * 32 + cnt] = p
                cnt = cnt + v
            counts[d, k] = cnt
    c1 = [counts[d, 1] for d in range(4)]
    c2 = [counts[d, 2] for d in range(4)]
    c3 = [counts[d, 3] for d in range(4)]

    def clamp(d, x):
        return jnp.minimum(jnp.maximum(x, jnp.maximum(0, c2[d] - FAR)), jnp.minimum(FAR, c2[d]))

    def worst(a):
        top = jnp.int32(0)
        for s in range(4):
            d1, d2, u1 = (s - 1) % 4, (s - 2) % 4, (s + 1) % 4
            down = jnp.maximum(OPEN, a[d2] + c1[d1]) + a[d1]
            up = jnp.maximum(OPEN, c2[d2] - a[d2] + c3[u1]) + c2[u1] - a[u1]
            top = jnp.maximum(top, jnp.maximum(down, up))
        return top

    a = [clamp(d, lax.shift_right_arithmetic(c2[d] + c3[d] - c1[d] + 1, 1)) for d in range(4)]
    for d in range(4):
        b = [c2[e] - a[e] for e in range(4)]

        def down(s):
            return a[(s - 2) % 4] + c1[(s - 1) % 4] + a[(s - 1) % 4]

        def up(s):
            return b[(s + 2) % 4] + c3[(s + 1) % 4] + b[(s + 1) % 4]

        m = jnp.maximum(down((d + 2) % 4), down((d + 1) % 4)) - a[d]
        n = jnp.maximum(up((d + 2) % 4), up((d + 3) % 4)) - b[d]
        a[d] = clamp(d, lax.shift_right_arithmetic(n + c2[d] - m + 1, 1))
    top = worst(a)
    half = [lax.shift_right_logical(c2[d] + 1, 1) for d in range(4)]
    fits = top <= CAPACITY
    a = [jnp.where(fits, a[d], half[d]) for d in range(4)]
    top = jnp.where(fits, top, CAPACITY)
    b = [c2[d] - a[d] for d in range(4)]

    def at(values, index):
        index = lax.rem(index + 8, 4)
        out = values[3]
        for i in range(3):
            out = jnp.where(index == i, values[i], out)
        return out

    def entry(row, i):
        v = lists[row + i]
        return jnp.minimum(jnp.maximum(v, 0), CHIP - 1)

    d1, d2, u1 = lax.rem(chip + 3, 4), lax.rem(chip + 2, 4), lax.rem(chip + 1, 4)
    far_row = (d2 * 4 + 2) * 32
    a_far, b_far = at(a, d2), at(b, d2)
    down_fwd = jnp.maximum(OPEN, a_far + at(c1, d1))
    up_fwd = jnp.maximum(OPEN, b_far + at(c3, u1))
    for i in range(CAPACITY):
        plan_ref[i] = 0
        plan_ref[CAPACITY + i] = 0
    for i in range(FAR):
        plan_ref[i] = entry(far_row, i)
        plan_ref[CAPACITY + i] = entry(far_row, a_far + i)
    for i in range(PART):
        plan_ref[a_far + i] = entry((d1 * 4 + 1) * 32, i)
        plan_ref[CAPACITY + b_far + i] = entry((u1 * 4 + 3) * 32, i)
    for i in range(FAR):
        plan_ref[down_fwd + i] = CHIP + i
        plan_ref[CAPACITY + up_fwd + i] = CHIP + i

    own_a = at(a, chip)
    from_up = at(a, chip + 3)
    from_down = at(b, chip + 1)
    far_down = jnp.maximum(OPEN, at(a, chip + 3) + at(c1, chip))
    far_up = jnp.maximum(OPEN, at(b, chip + 1) + at(c3, chip))
    for j in range(PART):
        old = anc_ref[member * PART + j]
        src = third(old)
        k = lax.rem(src - chip + 4, 4)
        r = ranks[chip * 96 + old]
        far = jnp.where(r < own_a, CHIP + far_down + r, CHIP + CAPACITY + far_up + r - own_a)
        where = jnp.where(
            k == 0,
            old - src * CHIP,
            jnp.where(
                k == 1,
                CHIP + from_up + r,
                jnp.where(k == 3, CHIP + CAPACITY + from_down + r, far),
            ),
        )
        plan_ref[GATHER_AT + j] = where
    level = jnp.int32(0)
    for size in LEVELS[:-1]:
        level = level + jnp.where(top > size, 1, 0)
    level_ref[0] = level


def make_plan(ancestors):
    return pl.pallas_call(
        plan_kernel,
        out_shape=(jax.ShapeDtypeStruct((64,), jnp.int32), jax.ShapeDtypeStruct((1,), jnp.int32)),
        in_specs=[pl.BlockSpec(memory_space=pltpu.SMEM)],
        out_specs=(pl.BlockSpec(memory_space=pltpu.SMEM), pl.BlockSpec(memory_space=pltpu.SMEM)),
        scratch_shapes=[
            pltpu.SMEM((4 * 96,), jnp.int32),
            pltpu.SMEM((4 * 96,), jnp.int32),
            pltpu.SMEM((16 * 32,), jnp.int32),
        ],
    )(ancestors)


def one_step(u, v, h, cor, obs, nud, force):
    rows, lanes = u.shape
    row = lax.broadcasted_iota(jnp.int32, u.shape, 0)

    def across(q):
        return pltpu.roll(q, lanes - 1, 1) - pltpu.roll(q, 1, 1)

    def along(q):
        above = jnp.where(row == rows - 1, 0.0, pltpu.roll(q, rows - 1, 0))
        below = jnp.where(row == 0, 0.0, pltpu.roll(q, 1, 0))
        return above - below

    u_new = u + cor * v - 0.125 * across(h)
    v_new = v - cor * u - 0.125 * along(h)
    h_new = h - 0.125 * (across(u_new) + along(v_new)) + nud * (obs - h) + force
    return u_new, v_new, h_new


def cycle_kernel(
    size, plan, ens_hbm, pert_hbm, obs_hbm, prec_hbm, nud_hbm,
    slots, lw_out,
    ens, pert, fields, cor_v, pool, first, stage, msg_out, msg_in, win, edge,
    misfit, zbuf, xbuf, lwbuf,
    in_sem, const_sem, halo_send, halo_recv, pool_send, pool_recv,
    edge_sem, ring_send, ring_recv, mir_send, mir_recv, out_sem,
    z_send, z_recv, x_send, x_recv, m_send, m_recv,
):
    member, lon = lax.axis_index("member"), lax.axis_index("lon")
    core = lax.rem(member, 2)
    lon_x, lon_z = lax.div(lon, 4), lax.rem(lon, 4)
    sibling = {"member": member + 1 - 2 * core}
    ring = ({"member": lax.rem(member + 6, 8)}, {"member": lax.rem(member + 2, 8)})
    sides = ({"lon": lax.rem(lon + 15, 16)}, {"lon": lax.rem(lon + 1, 16)})
    z_peers = [{"lon": lon_x * 4 + lax.rem(lon_z + k, 4)} for k in range(1, 4)]
    x_peers = [{"lon": lax.rem(lon_x + k, 4) * 4 + lon_z} for k in range(1, 4)]
    m_peers = [{"member": lax.rem(member + k, 8)} for k in range(1, 8)]

    def remote(src, dst, ssem, rsem, to):
        return pltpu.make_async_remote_copy(
            src_ref=src, dst_ref=dst, send_sem=ssem, recv_sem=rsem, device_id=to, device_id_type=MESH
        )

    loads = []
    for g in range(3):
        part = pl.ds(4 * g, 4)
        loads.append((
            pltpu.make_async_copy(ens_hbm.at[part], ens.at[part], in_sem.at[0, g]),
            pltpu.make_async_copy(pert_hbm.at[part], pert.at[part], in_sem.at[1, g]),
        ))
    consts = [
        pltpu.make_async_copy(ref, fields.at[i], const_sem.at[i])
        for i, ref in enumerate((obs_hbm, prec_hbm, nud_hbm))
    ]
    for cp in consts:
        cp.start()
    for pair in loads:
        for cp in pair:
            cp.start()

    barrier = pltpu.get_barrier_semaphore()
    everyone = list(sides) + z_peers + x_peers + m_peers
    for peer in everyone:
        pl.semaphore_signal(barrier, inc=1, device_id=peer, device_id_type=MESH)

    row_at = lax.broadcasted_iota(jnp.int32, (LAT, 128), 0).astype(F32)
    cor_v[...] = 0.3 * jnp.sin(math.pi * (row_at + 0.5 - LAT / 2) / LAT)

    for cp in consts:
        cp.wait()
    for pair in loads:
        for cp in pair:
            cp.wait()

    lane = lax.broadcasted_iota(jnp.int32, (LAT, 128), 1)

    def tile(which, p, side):
        cut = slice(0, 128) if side == 0 else slice(128, 256)
        if which < 3:
            return ens[p, which, :, cut]
        if which < 6:
            return pert[p, which - 3, :, cut]
        return fields[0 if which == 6 else 2, :, cut]

    def turned(x, by):
        by = by % 128
        return x if by == 0 else pltpu.roll(x, by, 1)

    def item(which, p):
        i = which * PART + p if which < 5 else (60 if which == 6 else 61)
        return i // 21, 6 * (i % 21)

    items = [(f, p) for f in range(5) for p in range(PART)] + [(6, 0), (7, 0)]
    for side in range(2):
        start = 0 if side == 0 else 122
        acc = [None] * 3
        for f, p in items:
            t, o = item(f, p)
            x = turned(tile(f, p, side), o - start)
            acc[t] = x if acc[t] is None else jnp.where(lane >= o, x, acc[t])
        for t in range(3):
            msg_out[side, t] = acc[t]

    pl.semaphore_wait(barrier, len(everyone))
    halos = [
        remote(msg_out.at[s], msg_in.at[1 - s], halo_send.at[s], halo_recv.at[1 - s], sides[s])
        for s in range(2)
    ]
    for cp in halos:
        cp.start()

    def share(at, p):
        return remote(pool.at[at], pool.at[at], pool_send.at[p], pool_recv.at[p], sibling)

    def interior(p, carry):
        cor = jnp.concatenate([cor_v[...], cor_v[...]], axis=1)
        u, v, h = ens[p, 0], ens[p, 1], ens[p, 2]
        for step in range(STEPS):
            u, v, h = one_step(u, v, h, cor, fields[0], fields[2], pert[p, step])
        at = core * PART + p
        pool[at, 0], pool[at, 1], pool[at, 2] = u, v, h
        share(at, p).start()
        return carry

    lax.fori_loop(0, PART, interior, 0)

    for s in range(2):
        remote(msg_out.at[s], msg_in.at[s], halo_send.at[s], halo_recv.at[s], sides[s]).wait_recv()
    for s in range(2):
        for half in range(2):
            members = list(range(half * PER_TILE, min(PART, (half + 1) * PER_TILE)))
            for f in range(8):
                if f >= 6 and half == 1:
                    continue
                count = PER_TILE if f >= 6 else len(members)
                acc = None
                for q in range(count):
                    p = members[q] if f < 6 else 0
                    o = WIN * q
                    if s == 0:
                        own, own_o = turned(tile(f, p, 0), o + HALO), o + HALO
                        nb_o = o
                    else:
                        own, own_o = turned(tile(f, p, 1), o - 116), o
                        nb_o = o + 2 * HALO
                    parts = [(own_o, own)]
                    if f != 5:
                        t, io = item(f, p)
                        nb = turned(msg_in[s, t], nb_o - io)
                        parts.append((nb_o, nb))
                    parts.sort(key=lambda e: e[0])
                    for off, x in parts:
                        acc = x if acc is None else jnp.where(lane >= off, x, acc)
                win[s, half, f] = acc
    for s in range(2):
        for half in range(2):
            u, v, h = win[s, half, 0], win[s, half, 1], win[s, half, 2]
            for step in range(STEPS):
                u, v, h = one_step(u, v, h, cor_v[...], win[s, 0, 6], win[s, 0, 7], win[s, half, 3 + step])
            edge[core, s, half, 0], edge[core, s, half, 1], edge[core, s, half, 2] = u, v, h

    edge_copy = remote(edge.at[core], edge.at[core], edge_sem.at[0], edge_sem.at[1], sibling)
    edge_copy.start()
    for p in range(PART):
        share((1 - core) * PART + p, p).wait_recv()
    remote(edge.at[1 - core], edge.at[1 - core], edge_sem.at[0], edge_sem.at[1], sibling).wait_recv()

    def whole(i):
        on = jnp.where(i >= PART, 1, 0)
        p = i - on * PART
        half = jnp.where(p >= PER_TILE, 1, 0)
        back = 128 - HALO - WIN * (p - half * PER_TILE)
        out = []
        for f in range(3):
            left = pltpu.roll(edge[on, 0, half, f], back, 1)
            right = pltpu.roll(edge[on, 1, half, f], back - HALO, 1)
            low = jnp.where(lane < HALO, left, pool[i, f, :, 0:128])
            high = jnp.where(lane >= 128 - HALO, right, pool[i, f, :, 128:256])
            out.append((low, high))
        return out

    positions = (size + 1) // 2
    open_pos, far_pos = OPEN // 2, FAR // 2

    def split(pos):
        return 2 * pos + 1 == size

    def entry_at(pos, on_core):
        return 2 * pos if split(pos) else 2 * pos + on_core

    def rows(ref, pos, on_core):
        return ref.at[:, pl.ds(on_core * (LAT // 2), LAT // 2), :] if split(pos) else ref

    def landing(way, pos, on_core):
        i = entry_at(pos, on_core)
        if pos < far_pos:
            return first.at[way, i]
        return rows(slots.at[CHIP + way * CAPACITY + i], pos, on_core)

    def ring_copy(way, pos):
        return remote(
            rows(stage.at[way, pos], pos, core), landing(way, pos, core),
            ring_send.at[way, pos], ring_recv.at[way, pos], ring[way],
        )

    def mirror_copy(way, pos, on_core):
        ref = landing(way, pos, on_core)
        return remote(ref, ref, mir_send.at[way, pos], mir_recv.at[way, pos], sibling)

    for pos in range(open_pos):
        for way in range(2):
            parts = whole(plan[way * CAPACITY + entry_at(pos, core)])
            for f in range(3):
                stage[way, pos, f, :, 0:128], stage[way, pos, f, :, 128:256] = parts[f]
            ring_copy(way, pos).start()

    for p in range(PART):
        share(core * PART + p, p).wait_send()

    def complete(i, carry):
        parts = whole(i)
        for f in range(3):
            pool[i, f, :, 0:128], pool[i, f, :, 128:256] = parts[f]
        lo = fields[0, :, 0:128] - parts[2][0]
        hi = fields[0, :, 128:256] - parts[2][1]
        term = fields[1, :, 0:128] * lo * lo + fields[1, :, 128:256] * hi * hi
        misfit[i] = jnp.sum(term.reshape(LAT // 8, 8, 128), axis=0)
        return carry

    lax.fori_loop(0, CHIP, complete, 0)
    keep = [pltpu.make_async_copy(pool, slots.at[pl.ds(0, CHIP)], out_sem.at[0])]
    keep[0].start()

    total = jnp.sum(jnp.sum(misfit[pl.ds(core * PART, PART)], axis=1), axis=1, keepdims=True)
    small = lax.broadcasted_iota(jnp.int32, (PART, 128), 1)
    which = lax.broadcasted_iota(jnp.int32, (PART, 128), 0)
    line = jnp.sum(jnp.where(small == which, total, 0.0), axis=0, keepdims=True)
    zbuf[lon_z] = jnp.broadcast_to(line, (8, 128))
    z_copies = [
        remote(zbuf.at[lon_z], zbuf.at[lon_z], z_send.at[k], z_recv.at[k], z_peers[k]) for k in range(3)
    ]
    for cp in z_copies:
        cp.start()

    for k in range(3):
        z_copies[k].wait_send()
        z_copies[k].wait_recv()
    xbuf[lon_x] = ((zbuf[0] + zbuf[1]) + zbuf[2]) + zbuf[3]
    x_copies = [
        remote(xbuf.at[lon_x], xbuf.at[lon_x], x_send.at[k], x_recv.at[k], x_peers[k]) for k in range(3)
    ]
    for cp in x_copies:
        cp.start()
    for cp in x_copies:
        cp.wait_send()
        cp.wait_recv()
    lwbuf[member] = ((xbuf[0] + xbuf[1]) + xbuf[2]) + xbuf[3]
    m_copies = [
        remote(lwbuf.at[member], lwbuf.at[member], m_send.at[k], m_recv.at[k], m_peers[k]) for k in range(7)
    ]
    for cp in m_copies:
        cp.start()

    for pos in range(far_pos):
        for way in range(2):
            ring_copy(way, pos).wait_recv()
            mirror_copy(way, pos, core).start()
    for pos in range(far_pos):
        for way in range(2):
            mirror_copy(way, pos, 1 - core).wait_recv()
    for way in range(2):
        cp = pltpu.make_async_copy(
            first.at[way], slots.at[pl.ds(CHIP + way * CAPACITY, FAR)], out_sem.at[1 + way]
        )
        cp.start()
        keep.append(cp)
    for pos in range(open_pos, positions):
        for way in range(2):
            idx = plan[way * CAPACITY + entry_at(pos, core)]
            own = pool[jnp.minimum(idx, CHIP - 1)]
            passed = first[way, jnp.clip(idx - CHIP, 0, FAR - 1)]
            stage[way, pos] = jnp.where(idx < CHIP, own, passed)
            ring_copy(way, pos).start()
    for pos in range(far_pos, positions):
        for way in range(2):
            ring_copy(way, pos).wait_recv()
            mirror_copy(way, pos, core).start()

    for cp in m_copies:
        cp.wait_send()
        cp.wait_recv()
    lw_out[...] = lwbuf[...]
    for cp in halos + [edge_copy]:
        cp.wait_send()
    for pos in range(positions):
        for way in range(2):
            ring_copy(way, pos).wait_send()
    for pos in range(positions):
        for way in range(2):
            mirror_copy(way, pos, core).wait_send()
            if pos >= far_pos:
                mirror_copy(way, pos, 1 - core).wait_recv()
    for cp in keep:
        cp.wait()


def run_cycle(size, number, plan, ensemble, perturbation, observed, precision, nudging):
    anywhere = pl.BlockSpec(memory_space=pltpu.HBM)
    dma = pltpu.SemaphoreType.DMA
    most = (size + 1) // 2
    return pl.pallas_call(
        functools.partial(cycle_kernel, size),
        out_shape=(
            jax.ShapeDtypeStruct((SLOTS, 3, LAT, CLON), F32),
            jax.ShapeDtypeStruct((8, 8, 128), F32),
        ),
        in_specs=[pl.BlockSpec(memory_space=pltpu.SMEM)] + [anywhere] * 5,
        out_specs=(anywhere, pl.BlockSpec(memory_space=pltpu.VMEM)),
        scratch_shapes=[
            pltpu.VMEM((PART, 3, LAT, CLON), F32),
            pltpu.VMEM((PART, 3, LAT, CLON), F32),
            pltpu.VMEM((3, LAT, CLON), F32),
            pltpu.VMEM((LAT, 128), F32),
            pltpu.VMEM((CHIP, 3, LAT, CLON), F32),
            pltpu.VMEM((2, FAR, 3, LAT, CLON), F32),
            pltpu.VMEM((2, most, 3, LAT, CLON), F32),
            pltpu.VMEM((2, 3, LAT, 128), F32),
            pltpu.VMEM((2, 3, LAT, 128), F32),
            pltpu.VMEM((2, 2, 8, LAT, 128), F32),
            pltpu.VMEM((2, 2, 2, 3, LAT, 128), F32),
            pltpu.VMEM((CHIP, 8, 128), F32),
            pltpu.VMEM((4, 8, 128), F32),
            pltpu.VMEM((4, 8, 128), F32),
            pltpu.VMEM((8, 8, 128), F32),
            dma((2, 3)), dma((3,)), dma((2,)), dma((2,)), dma((PART,)), dma((PART,)), dma((2,)),
            dma((2, most)), dma((2, most)), dma((2, most)), dma((2, most)), dma((3,)),
            dma((3,)), dma((3,)), dma((3,)), dma((3,)), dma((7,)), dma((7,)),
        ],
        compiler_params=pltpu.CompilerParams(
            collective_id=number, has_side_effects=True, vmem_limit_bytes=50 * 2**20
        ),
    )(plan, ensemble, perturbation, observed, precision, nudging)


def resample_kernel(plan, lw_ref, slots, weights_ref, analysis, held, in_sem, out_sem):
    ins = [
        pltpu.make_async_copy(slots.at[plan[GATHER_AT + j]], held.at[j], in_sem.at[j]) for j in range(PART)
    ]
    outs = [pltpu.make_async_copy(held.at[j], analysis.at[j], out_sem.at[j]) for j in range(PART)]
    for cp in ins:
        cp.start()
    lane = lax.broadcasted_iota(jnp.int32, (8, 8, 128), 2)
    logw = jnp.where(lane < PART, lw_ref[...] * (-2.0 / (LAT * CLON * 16)), -jnp.inf)
    top = jnp.max(jnp.max(logw, axis=0), axis=1, keepdims=True)
    e = jnp.exp(logw - top[None])
    whole = jnp.sum(jnp.sum(e, axis=0), axis=1, keepdims=True)
    own = jnp.where(
        lax.broadcasted_iota(jnp.int32, (8, 8, 128), 0) == lax.axis_index("member"), e, 0.0
    )
    row = jnp.sum(own, axis=0) / whole
    weights_ref[...] = row[0, :PART]
    for j in range(PART):
        ins[j].wait()
        outs[j].start()
    for cp in outs:
        cp.wait()


def resample(plan, lw, slots):
    return pl.pallas_call(
        resample_kernel,
        out_shape=(
            jax.ShapeDtypeStruct((PART,), F32),
            jax.ShapeDtypeStruct((PART, 3, LAT, CLON), F32),
        ),
        in_specs=[
            pl.BlockSpec(memory_space=pltpu.SMEM),
            pl.BlockSpec(memory_space=pltpu.VMEM),
            pl.BlockSpec(memory_space=pltpu.HBM),
        ],
        out_specs=(pl.BlockSpec(memory_space=pltpu.VMEM), pl.BlockSpec(memory_space=pltpu.HBM)),
        scratch_shapes=[
            pltpu.VMEM((PART, 3, LAT, CLON), F32),
            pltpu.SemaphoreType.DMA((PART,)),
            pltpu.SemaphoreType.DMA((PART,)),
        ],
    )(plan, lw, slots)


def body(ensemble, perturbation, observed, precision, nudging, ancestors):
    plan, level = make_plan(ancestors)
    operands = (plan, ensemble, perturbation, observed, precision, nudging)
    branches = [functools.partial(run_cycle, size, n) for n, size in enumerate(LEVELS)]
    if len(branches) == 1:
        slots, lw = branches[0](*operands)
    else:
        slots, lw = lax.switch(level.reshape(()), branches, *operands)
    weights, analysis = resample(plan, lw, slots)
    return weights, analysis


def solution(mesh):
    placed = (
        P("member", None, None, "lon"),
        P("member", None, None, "lon"),
        P(None, "lon"),
        P(None, "lon"),
        P(None, "lon"),
        P(),
    )
    return jax.shard_map(
        body,
        mesh=mesh,
        in_specs=placed,
        out_specs=(P("member"), P("member", None, None, "lon")),
        check_vma=False,
    )
```

```python
import functools
import math

import jax
import jax.numpy as jnp
from jax import lax
from jax.experimental import pallas as pl
from jax.experimental.pallas import tpu as pltpu
from jax.sharding import PartitionSpec as P

MESH = pl.DeviceIdType.MESH
F32 = jnp.float32
STEPS = 3
LAT = 64
CLON = 256
PART = 12
CHIP = 24
HALO = 6
STRIDE = 32
GROUP = 4
TILES = PART // GROUP
PIECES = ((2, 6, 0), (0, 5, 6), (1, 5, 11), (3, 4, 16), (4, 2, 20), (6, 4, 22), (7, 4, 26))
FAR = 6
OPEN = 8
CAPACITY = 24
LEVELS = (12, 13, 14, 16, 24)
SLOTS = CHIP + 2 * CAPACITY
GATHER_AT = 2 * CAPACITY


def plan_kernel(anc_ref, plan_ref, level_ref, need, ranks, lists):
    member = lax.axis_index("member")
    chip = lax.div(member, 2)

    def third(a):
        return lax.shift_right_logical(a * 2731, 16)

    for i in range(4 * 96):
        need[i] = 0
    for j in range(96):
        need[(j // CHIP) * 96 + anc_ref[j]] = 1
    counts = {}
    for d in range(4):
        for k in range(1, 4):
            s = (d + k) % 4
            cnt = jnp.int32(0)
            for p in range(CHIP):
                v = need[d * 96 + s * CHIP + p]
                ranks[d * 96 + s * CHIP + p] = cnt
                lists[(d * 4 + k) * 32 + cnt] = p
                cnt = cnt + v
            counts[d, k] = cnt
    c1 = [counts[d, 1] for d in range(4)]
    c2 = [counts[d, 2] for d in range(4)]
    c3 = [counts[d, 3] for d in range(4)]

    def clamp(d, x):
        return jnp.minimum(jnp.maximum(x, jnp.maximum(0, c2[d] - FAR)), jnp.minimum(FAR, c2[d]))

    def worst(a):
        top = jnp.int32(0)
        for s in range(4):
            d1, d2, u1 = (s - 1) % 4, (s - 2) % 4, (s + 1) % 4
            down = jnp.maximum(OPEN, a[d2] + c1[d1]) + a[d1]
            up = jnp.maximum(OPEN, c2[d2] - a[d2] + c3[u1]) + c2[u1] - a[u1]
            top = jnp.maximum(top, jnp.maximum(down, up))
        return top

    a = [clamp(d, lax.shift_right_arithmetic(c2[d] + c3[d] - c1[d] + 1, 1)) for d in range(4)]
    for d in range(4):
        b = [c2[e] - a[e] for e in range(4)]

        def down(s):
            return a[(s - 2) % 4] + c1[(s - 1) % 4] + a[(s - 1) % 4]

        def up(s):
            return b[(s + 2) % 4] + c3[(s + 1) % 4] + b[(s + 1) % 4]

        m = jnp.maximum(down((d + 2) % 4), down((d + 1) % 4)) - a[d]
        n = jnp.maximum(up((d + 2) % 4), up((d + 3) % 4)) - b[d]
        a[d] = clamp(d, lax.shift_right_arithmetic(n + c2[d] - m + 1, 1))
    top = worst(a)
    half = [lax.shift_right_logical(c2[d] + 1, 1) for d in range(4)]
    fits = top <= CAPACITY
    a = [jnp.where(fits, a[d], half[d]) for d in range(4)]
    top = jnp.where(fits, top, CAPACITY)
    b = [c2[d] - a[d] for d in range(4)]

    def at(values, index):
        index = lax.rem(index + 8, 4)
        out = values[3]
        for i in range(3):
            out = jnp.where(index == i, values[i], out)
        return out

    def entry(row, i):
        v = lists[row + i]
        return jnp.minimum(jnp.maximum(v, 0), CHIP - 1)

    d1, d2, u1 = lax.rem(chip + 3, 4), lax.rem(chip + 2, 4), lax.rem(chip + 1, 4)
    far_row = (d2 * 4 + 2) * 32
    a_far, b_far = at(a, d2), at(b, d2)
    down_fwd = jnp.maximum(OPEN, a_far + at(c1, d1))
    up_fwd = jnp.maximum(OPEN, b_far + at(c3, u1))
    for i in range(CAPACITY):
        plan_ref[i] = 0
        plan_ref[CAPACITY + i] = 0
    for i in range(FAR):
        plan_ref[i] = entry(far_row, i)
        plan_ref[CAPACITY + i] = entry(far_row, a_far + i)
    for i in range(PART):
        plan_ref[a_far + i] = entry((d1 * 4 + 1) * 32, i)
        plan_ref[CAPACITY + b_far + i] = entry((u1 * 4 + 3) * 32, i)
    for i in range(FAR):
        plan_ref[down_fwd + i] = CHIP + i
        plan_ref[CAPACITY + up_fwd + i] = CHIP + i

    own_a = at(a, chip)
    from_up = at(a, chip + 3)
    from_down = at(b, chip + 1)
    far_down = jnp.maximum(OPEN, at(a, chip + 3) + at(c1, chip))
    far_up = jnp.maximum(OPEN, at(b, chip + 1) + at(c3, chip))
    for j in range(PART):
        old = anc_ref[member * PART + j]
        src = third(old)
        k = lax.rem(src - chip + 4, 4)
        r = ranks[chip * 96 + old]
        far = jnp.where(r < own_a, CHIP + far_down + r, CHIP + CAPACITY + far_up + r - own_a)
        where = jnp.where(
            k == 0,
            old - src * CHIP,
            jnp.where(
                k == 1,
                CHIP + from_up + r,
                jnp.where(k == 3, CHIP + CAPACITY + from_down + r, far),
            ),
        )
        plan_ref[GATHER_AT + j] = where
    level = jnp.int32(0)
    for size in LEVELS[:-1]:
        level = level + jnp.where(top > size, 1, 0)
    level_ref[0] = level


def make_plan(ancestors):
    return pl.pallas_call(
        plan_kernel,
        out_shape=(jax.ShapeDtypeStruct((64,), jnp.int32), jax.ShapeDtypeStruct((1,), jnp.int32)),
        in_specs=[pl.BlockSpec(memory_space=pltpu.SMEM)],
        out_specs=(pl.BlockSpec(memory_space=pltpu.SMEM), pl.BlockSpec(memory_space=pltpu.SMEM)),
        scratch_shapes=[
            pltpu.SMEM((4 * 96,), jnp.int32),
            pltpu.SMEM((4 * 96,), jnp.int32),
            pltpu.SMEM((16 * 32,), jnp.int32),
        ],
    )(ancestors)


def one_step(u_at, v_at, h_at, h_rows, v_rows, put_u, put_v, put_h, cor, obs, nud, force, tiles):
    blocks = LAT // 8
    lane = lax.broadcasted_iota(jnp.int32, (8, 128), 1)
    lane_first, lane_last = lane == 0, lane == 127

    def across(q):
        after = [pltpu.roll(x, 127, 1) for x in q]
        before = [pltpu.roll(x, 1, 1) for x in q]
        if tiles == 1:
            return [after[0] - before[0]]
        return [
            jnp.where(lane_last, after[1], after[0]) - before[0],
            after[1] - jnp.where(lane_first, before[0], before[1]),
        ]

    def along(ref, r, t):
        return ref[t, pl.ds(8 * r + 9, 8), :] - ref[t, pl.ds(8 * r + 7, 8), :]

    dxu, centre = [], []

    def finish(r):
        for t in range(tiles):
            x = centre[r][t]
            put_h(
                r, t,
                x - 0.125 * (dxu[r][t] + along(v_rows, r, t)) + nud(r, t) * (obs(r, t) - x) + force(r, t),
            )

    for r in range(blocks):
        h = [h_at(r, t) for t in range(tiles)]
        centre.append(h)
        dxh = across(h)
        f = cor(r)
        u_new = []
        for t in range(tiles):
            u, v = u_at(r, t), v_at(r, t)
            u_new.append(u + f * v - 0.125 * dxh[t])
            v_new = v - f * u - 0.125 * along(h_rows, r, t)
            put_u(r, t, u_new[t])
            put_v(r, t, v_new)
            v_rows[t, 8 * r + 8:8 * r + 16, :] = v_new
        dxu.append(across(u_new))
        if r:
            finish(r - 1)
    finish(blocks - 1)


def block(ref, lead, r, t):
    return ref[(*lead, slice(8 * r, 8 * r + 8), slice(128 * t, 128 * t + 128))]


def put(ref, lead, r, t, x):
    ref[(*lead, slice(8 * r, 8 * r + 8), slice(128 * t, 128 * t + 128))] = x


def three_steps(start, result, hs, vs, us, cor_v, obs, nud, force, tiles):
    for r in range(LAT // 8):
        for t in range(tiles):
            hs[0, t, 8 * r + 8:8 * r + 16, :] = start(2, r, t)
    for step in range(STEPS):
        now, later, last = step % 2, (step + 1) % 2, step == STEPS - 1

        def padded(ref, at):
            return lambda r, t: ref[at, t, 8 * r + 8:8 * r + 16, :]

        def store(f, ref):
            def go(r, t, x):
                if last:
                    result(f, r, t, x)
                elif f != 1:
                    ref[later, t, 8 * r + 8:8 * r + 16, :] = x
            return go

        one_step(
            (lambda r, t: start(0, r, t)) if step == 0 else padded(us, now),
            (lambda r, t: start(1, r, t)) if step == 0 else padded(vs, now),
            padded(hs, now), hs.at[now], vs.at[later],
            store(0, us), store(1, vs), store(2, hs),
            lambda r: block(cor_v, (), r, 0), obs, nud, functools.partial(force, step), tiles,
        )


def cycle_kernel(
    size, plan, ens_hbm, pert_hbm, obs_hbm, prec_hbm, nud_hbm,
    slots, lw_out,
    ens, pert, fields, cor_v, pool, first, stage, msg_out, msg_in, edges, win, half, edge, hs, vs, us,
    misfit, zbuf, xbuf, lwbuf,
    in_sem, const_sem, halo_send, halo_recv, pool_send, pool_recv,
    edge_sem, ring_send, ring_recv, mir_send, mir_recv, out_sem,
    z_send, z_recv, x_send, x_recv, m_send, m_recv,
):
    member, lon = lax.axis_index("member"), lax.axis_index("lon")
    core = lax.rem(member, 2)
    lon_x, lon_z = lax.div(lon, 4), lax.rem(lon, 4)
    sibling = {"member": member + 1 - 2 * core}
    ring = ({"member": lax.rem(member + 6, 8)}, {"member": lax.rem(member + 2, 8)})
    sides = ({"lon": lax.rem(lon + 15, 16)}, {"lon": lax.rem(lon + 1, 16)})
    z_peers = [{"lon": lon_x * 4 + lax.rem(lon_z + k, 4)} for k in range(1, 4)]
    x_peers = [{"lon": lax.rem(lon_x + k, 4) * 4 + lon_z} for k in range(1, 4)]
    m_peers = [{"member": lax.rem(member + k, 8)} for k in range(1, 8)]

    def remote(src, dst, ssem, rsem, to):
        return pltpu.make_async_remote_copy(
            src_ref=src, dst_ref=dst, send_sem=ssem, recv_sem=rsem, device_id=to, device_id_type=MESH
        )

    loads = []
    for g in range(3):
        part = pl.ds(4 * g, 4)
        loads.append((
            pltpu.make_async_copy(ens_hbm.at[part], ens.at[part], in_sem.at[0, g]),
            pltpu.make_async_copy(pert_hbm.at[part], pert.at[part], in_sem.at[1, g]),
        ))
    consts = [
        pltpu.make_async_copy(ref, fields.at[i], const_sem.at[i])
        for i, ref in enumerate((obs_hbm, prec_hbm, nud_hbm))
    ]
    for cp in consts:
        cp.start()
    for pair in loads:
        for cp in pair:
            cp.start()

    barrier = pltpu.get_barrier_semaphore()
    everyone = list(sides) + z_peers + x_peers + m_peers
    for peer in everyone:
        pl.semaphore_signal(barrier, inc=1, device_id=peer, device_id_type=MESH)

    row_at = lax.broadcasted_iota(jnp.int32, (LAT, 128), 0).astype(F32)
    cor_v[...] = 0.3 * jnp.sin(math.pi * (row_at + 0.5 - LAT / 2) / LAT)

    for ref in (hs, vs):
        for n in range(2):
            for t in range(2):
                ref[n, t, 0:8, :] = jnp.zeros((8, 128), F32)
                ref[n, t, LAT + 8:LAT + 16, :] = jnp.zeros((8, 128), F32)

    for cp in consts:
        cp.wait()
    for pair in loads:
        for cp in pair:
            cp.wait()

    lane = lax.broadcasted_iota(jnp.int32, (LAT, 128), 1)

    def tile(which, p, side):
        cut = slice(0, 128) if side == 0 else slice(128, 256)
        if which < 3:
            return ens[p, which, :, cut]
        if which < 6:
            return pert[p, which - 3, :, cut]
        return fields[0 if which == 6 else 2, :, cut]

    def turned(x, by):
        by = by % 128
        return x if by == 0 else pltpu.roll(x, by, 1)

    within = lane & (STRIDE - 1)

    def outer(which, p, q):
        return turned(jnp.where(lane < 64, tile(which, p, 0), tile(which, p, 1)), STRIDE * q + HALO)

    for which in range(8):
        for group in range(TILES if which < 6 else 1):
            start = acc = outer(which, group * GROUP, 0)
            for q in range(1, GROUP):
                acc = jnp.where(lane >= STRIDE * q - HALO, outer(which, group * GROUP + q, q), acc)
            edges[which, group] = jnp.where(lane >= 128 - HALO, start, acc)

    def spot(which, group):
        return which, (group if which < 6 else 0)

    for side in range(2):
        for group in range(TILES):
            acc = None
            for which, width, to in PIECES:
                source = HALO if side == 0 else HALO - width
                x = turned(edges[spot(which, group)], to - source)
                acc = x if acc is None else jnp.where(within >= to, x, acc)
            msg_out[side, group] = acc

    pl.semaphore_wait(barrier, len(everyone))
    halos = [
        remote(msg_out.at[s], msg_in.at[1 - s], halo_send.at[s], halo_recv.at[1 - s], sides[s])
        for s in range(2)
    ]
    for cp in halos:
        cp.start()

    def share(at, p):
        return remote(pool.at[at], pool.at[at], pool_send.at[p], pool_recv.at[p], sibling)

    def interior(p, carry):
        at = core * PART + p
        three_steps(
            lambda f, r, t: block(ens, (p, f), r, t), lambda f, r, t, x: put(pool, (at, f), r, t, x),
            hs, vs, us, cor_v, lambda r, t: block(fields, (0,), r, t), lambda r, t: block(fields, (2,), r, t),
            lambda step, r, t: block(pert, (p, step), r, t), 2,
        )
        share(at, p).start()
        return carry

    lax.fori_loop(0, PART, interior, 0)

    for s in range(2):
        remote(msg_out.at[s], msg_in.at[s], halo_send.at[s], halo_recv.at[s], sides[s]).wait_recv()
    for s in range(2):
        for group in range(TILES):
            for which, width, at in PIECES:
                to = HALO - width if s == 0 else HALO
                x = turned(msg_in[s, group], to - at)
                inside = (within >= to) & (within < to + width)
                win[s, which, group] = jnp.where(inside, x, edges[spot(which, group)])
            win[s, 5, group] = edges[5, group]

    def edge_group(n, carry):
        for s in range(2):
            three_steps(
                lambda f, r, t: block(win, (s, f, n), r, t), lambda f, r, t, x: put(half, (s, f), r, t, x),
                hs, vs, us, cor_v, lambda r, t: block(win, (s, 6, n), r, t),
                lambda r, t: block(win, (s, 7, n), r, t), lambda step, r, t: block(win, (s, 3 + step, n), r, t), 1,
            )
        for f in range(3):
            edge[core, n, f] = jnp.where((within >= HALO) & (within < 2 * HALO), half[0, f], half[1, f])
        return carry

    lax.fori_loop(0, TILES, edge_group, 0)
    edge_copy = remote(edge.at[core], edge.at[core], edge_sem.at[0], edge_sem.at[1], sibling)
    edge_copy.start()
    for p in range(PART):
        share((1 - core) * PART + p, p).wait_recv()
    remote(edge.at[1 - core], edge.at[1 - core], edge_sem.at[0], edge_sem.at[1], sibling).wait_recv()

    def whole(i):
        on = jnp.where(i >= PART, 1, 0)
        p = i - on * PART
        group = lax.shift_right_logical(p, 2)
        back = 128 - HALO - STRIDE * (p - GROUP * group)
        out = []
        for f in range(3):
            x = pltpu.roll(edge[on, group, f], back, 1)
            low = jnp.where(lane < HALO, x, pool[i, f, :, 0:128])
            high = jnp.where(lane >= 128 - HALO, x, pool[i, f, :, 128:256])
            out.append((low, high))
        return out

    positions = (size + 1) // 2
    open_pos, far_pos = OPEN // 2, FAR // 2

    def split(pos):
        return 2 * pos + 1 == size

    def entry_at(pos, on_core):
        return 2 * pos if split(pos) else 2 * pos + on_core

    def rows(ref, pos, on_core):
        return ref.at[:, pl.ds(on_core * (LAT // 2), LAT // 2), :] if split(pos) else ref

    def landing(way, pos, on_core):
        i = entry_at(pos, on_core)
        if pos < far_pos:
            return first.at[way, i]
        return rows(slots.at[CHIP + way * CAPACITY + i], pos, on_core)

    def ring_copy(way, pos):
        return remote(
            rows(stage.at[way, pos], pos, core), landing(way, pos, core),
            ring_send.at[way, pos], ring_recv.at[way, pos], ring[way],
        )

    def mirror_copy(way, pos, on_core):
        ref = landing(way, pos, on_core)
        return remote(ref, ref, mir_send.at[way, pos], mir_recv.at[way, pos], sibling)

    for pos in range(open_pos):
        for way in range(2):
            parts = whole(plan[way * CAPACITY + entry_at(pos, core)])
            for f in range(3):
                stage[way, pos, f, :, 0:128], stage[way, pos, f, :, 128:256] = parts[f]
            ring_copy(way, pos).start()

    for p in range(PART):
        share(core * PART + p, p).wait_send()

    def complete(i, carry):
        parts = whole(i)
        for f in range(3):
            pool[i, f, :, 0:128], pool[i, f, :, 128:256] = parts[f]
        lo = fields[0, :, 0:128] - parts[2][0]
        hi = fields[0, :, 128:256] - parts[2][1]
        term = fields[1, :, 0:128] * lo * lo + fields[1, :, 128:256] * hi * hi
        misfit[i] = jnp.sum(term.reshape(LAT // 8, 8, 128), axis=0)
        return carry

    lax.fori_loop(0, CHIP, complete, 0)
    keep = [pltpu.make_async_copy(pool, slots.at[pl.ds(0, CHIP)], out_sem.at[0])]
    keep[0].start()

    total = jnp.sum(jnp.sum(misfit[pl.ds(core * PART, PART)], axis=1), axis=1, keepdims=True)
    small = lax.broadcasted_iota(jnp.int32, (PART, 128), 1)
    which = lax.broadcasted_iota(jnp.int32, (PART, 128), 0)
    line = jnp.sum(jnp.where(small == which, total, 0.0), axis=0, keepdims=True)
    zbuf[lon_z] = jnp.broadcast_to(line, (8, 128))
    z_copies = [
        remote(zbuf.at[lon_z], zbuf.at[lon_z], z_send.at[k], z_recv.at[k], z_peers[k]) for k in range(3)
    ]
    for cp in z_copies:
        cp.start()

    for k in range(3):
        z_copies[k].wait_send()
        z_copies[k].wait_recv()
    xbuf[lon_x] = ((zbuf[0] + zbuf[1]) + zbuf[2]) + zbuf[3]
    x_copies = [
        remote(xbuf.at[lon_x], xbuf.at[lon_x], x_send.at[k], x_recv.at[k], x_peers[k]) for k in range(3)
    ]
    for cp in x_copies:
        cp.start()
    for cp in x_copies:
        cp.wait_send()
        cp.wait_recv()
    lwbuf[member] = ((xbuf[0] + xbuf[1]) + xbuf[2]) + xbuf[3]
    m_copies = [
        remote(lwbuf.at[member], lwbuf.at[member], m_send.at[k], m_recv.at[k], m_peers[k]) for k in range(7)
    ]
    for cp in m_copies:
        cp.start()

    for pos in range(far_pos):
        for way in range(2):
            ring_copy(way, pos).wait_recv()
            mirror_copy(way, pos, core).start()
    for pos in range(far_pos):
        for way in range(2):
            mirror_copy(way, pos, 1 - core).wait_recv()
    for way in range(2):
        cp = pltpu.make_async_copy(
            first.at[way], slots.at[pl.ds(CHIP + way * CAPACITY, FAR)], out_sem.at[1 + way]
        )
        cp.start()
        keep.append(cp)
    for pos in range(open_pos, positions):
        for way in range(2):
            idx = plan[way * CAPACITY + entry_at(pos, core)]
            own = pool[jnp.minimum(idx, CHIP - 1)]
            passed = first[way, jnp.clip(idx - CHIP, 0, FAR - 1)]
            stage[way, pos] = jnp.where(idx < CHIP, own, passed)
            ring_copy(way, pos).start()
    for pos in range(far_pos, positions):
        for way in range(2):
            ring_copy(way, pos).wait_recv()
            mirror_copy(way, pos, core).start()

    for cp in m_copies:
        cp.wait_send()
        cp.wait_recv()
    lw_out[...] = lwbuf[...]
    for cp in halos + [edge_copy]:
        cp.wait_send()
    for pos in range(positions):
        for way in range(2):
            ring_copy(way, pos).wait_send()
    for pos in range(positions):
        for way in range(2):
            mirror_copy(way, pos, core).wait_send()
            if pos >= far_pos:
                mirror_copy(way, pos, 1 - core).wait_recv()
    for cp in keep:
        cp.wait()


def run_cycle(size, number, plan, ensemble, perturbation, observed, precision, nudging):
    anywhere = pl.BlockSpec(memory_space=pltpu.HBM)
    dma = pltpu.SemaphoreType.DMA
    most = (size + 1) // 2
    return pl.pallas_call(
        functools.partial(cycle_kernel, size),
        out_shape=(
            jax.ShapeDtypeStruct((SLOTS, 3, LAT, CLON), F32),
            jax.ShapeDtypeStruct((8, 8, 128), F32),
        ),
        in_specs=[pl.BlockSpec(memory_space=pltpu.SMEM)] + [anywhere] * 5,
        out_specs=(anywhere, pl.BlockSpec(memory_space=pltpu.VMEM)),
        scratch_shapes=[
            pltpu.VMEM((PART, 3, LAT, CLON), F32),
            pltpu.VMEM((PART, 3, LAT, CLON), F32),
            pltpu.VMEM((3, LAT, CLON), F32),
            pltpu.VMEM((LAT, 128), F32),
            pltpu.VMEM((CHIP, 3, LAT, CLON), F32),
            pltpu.VMEM((2, FAR, 3, LAT, CLON), F32),
            pltpu.VMEM((2, most, 3, LAT, CLON), F32),
            pltpu.VMEM((2, 3, LAT, 128), F32),
            pltpu.VMEM((2, 3, LAT, 128), F32),
            pltpu.VMEM((8, TILES, LAT, 128), F32),
            pltpu.VMEM((2, 8, TILES, LAT, 128), F32),
            pltpu.VMEM((2, 3, LAT, 128), F32),
            pltpu.VMEM((2, TILES, 3, LAT, 128), F32),
            pltpu.VMEM((2, 2, LAT + 16, 128), F32),
            pltpu.VMEM((2, 2, LAT + 16, 128), F32),
            pltpu.VMEM((2, 2, LAT + 16, 128), F32),
            pltpu.VMEM((CHIP, 8, 128), F32),
            pltpu.VMEM((4, 8, 128), F32),
            pltpu.VMEM((4, 8, 128), F32),
            pltpu.VMEM((8, 8, 128), F32),
            dma((2, 3)), dma((3,)), dma((2,)), dma((2,)), dma((PART,)), dma((PART,)), dma((2,)),
            dma((2, most)), dma((2, most)), dma((2, most)), dma((2, most)), dma((3,)),
            dma((3,)), dma((3,)), dma((3,)), dma((3,)), dma((7,)), dma((7,)),
        ],
        compiler_params=pltpu.CompilerParams(
            collective_id=number, has_side_effects=True, vmem_limit_bytes=50 * 2**20
        ),
    )(plan, ensemble, perturbation, observed, precision, nudging)


def resample_kernel(plan, lw_ref, slots, weights_ref, analysis, held, in_sem, out_sem):
    ins = [
        pltpu.make_async_copy(slots.at[plan[GATHER_AT + j]], held.at[j], in_sem.at[j]) for j in range(PART)
    ]
    outs = [pltpu.make_async_copy(held.at[j], analysis.at[j], out_sem.at[j]) for j in range(PART)]
    for cp in ins:
        cp.start()
    lane = lax.broadcasted_iota(jnp.int32, (8, 8, 128), 2)
    logw = jnp.where(lane < PART, lw_ref[...] * (-2.0 / (LAT * CLON * 16)), -jnp.inf)
    top = jnp.max(jnp.max(logw, axis=0), axis=1, keepdims=True)
    e = jnp.exp(logw - top[None])
    whole = jnp.sum(jnp.sum(e, axis=0), axis=1, keepdims=True)
    own = jnp.where(
        lax.broadcasted_iota(jnp.int32, (8, 8, 128), 0) == lax.axis_index("member"), e, 0.0
    )
    row = jnp.sum(own, axis=0) / whole
    weights_ref[...] = row[0, :PART]
    for j in range(PART):
        ins[j].wait()
        outs[j].start()
    for cp in outs:
        cp.wait()


def resample(plan, lw, slots):
    return pl.pallas_call(
        resample_kernel,
        out_shape=(
            jax.ShapeDtypeStruct((PART,), F32),
            jax.ShapeDtypeStruct((PART, 3, LAT, CLON), F32),
        ),
        in_specs=[
            pl.BlockSpec(memory_space=pltpu.SMEM),
            pl.BlockSpec(memory_space=pltpu.VMEM),
            pl.BlockSpec(memory_space=pltpu.HBM),
        ],
        out_specs=(pl.BlockSpec(memory_space=pltpu.VMEM), pl.BlockSpec(memory_space=pltpu.HBM)),
        scratch_shapes=[
            pltpu.VMEM((PART, 3, LAT, CLON), F32),
            pltpu.SemaphoreType.DMA((PART,)),
            pltpu.SemaphoreType.DMA((PART,)),
        ],
    )(plan, lw, slots)


def body(ensemble, perturbation, observed, precision, nudging, ancestors):
    plan, level = make_plan(ancestors)
    operands = (plan, ensemble, perturbation, observed, precision, nudging)
    branches = [functools.partial(run_cycle, size, n) for n, size in enumerate(LEVELS)]
    if len(branches) == 1:
        slots, lw = branches[0](*operands)
    else:
        slots, lw = lax.switch(level.reshape(()), branches, *operands)
    weights, analysis = resample(plan, lw, slots)
    return weights, analysis


def solution(mesh):
    placed = (
        P("member", None, None, "lon"),
        P("member", None, None, "lon"),
        P(None, "lon"),
        P(None, "lon"),
        P(None, "lon"),
        P(),
    )
    return jax.shard_map(
        body,
        mesh=mesh,
        in_specs=placed,
        out_specs=(P("member"), P("member", None, None, "lon")),
        check_vma=False,
    )
```

```python
import functools
import math

import jax
import jax.numpy as jnp
from jax import lax
from jax.experimental import pallas as pl
from jax.experimental.pallas import tpu as pltpu
from jax.sharding import PartitionSpec as P

MESH = pl.DeviceIdType.MESH
F32 = jnp.float32
STEPS = 3
LAT = 64
CLON = 256
PART = 12
CHIP = 24
HALO = 6
STRIDE = 32
GROUP = 4
TILES = PART // GROUP
PIECES = ((2, 6, 0), (0, 5, 6), (1, 5, 11), (3, 4, 16), (4, 2, 20), (6, 4, 22), (7, 4, 26))
CAPACITY = 24
WIDE = (CAPACITY, 6, 8)
NARROW = (4, 6)
LEVELS = tuple((size, *NARROW) for size in (11, 12, 13, 14, 16)) + (WIDE,)
SLOTS = CHIP + 2 * CAPACITY
GATHER_AT = 2 * CAPACITY


def plan_kernel(anc_ref, plan_ref, level_ref, need, ranks, lists):
    member = lax.axis_index("member")
    chip = lax.div(member, 2)

    def third(a):
        return lax.shift_right_logical(a * 2731, 16)

    for i in range(4 * 96):
        need[i] = 0
    for j in range(96):
        need[(j // CHIP) * 96 + anc_ref[j]] = 1
    counts = {}
    for d in range(4):
        for k in range(1, 4):
            s = (d + k) % 4
            cnt = jnp.int32(0)
            for p in range(CHIP):
                v = need[d * 96 + s * CHIP + p]
                ranks[d * 96 + s * CHIP + p] = cnt
                lists[(d * 4 + k) * 32 + cnt] = p
                cnt = cnt + v
            counts[d, k] = cnt
    c1 = [counts[d, 1] for d in range(4)]
    c2 = [counts[d, 2] for d in range(4)]
    c3 = [counts[d, 3] for d in range(4)]

    limit, free = NARROW

    def clamp(d, x):
        return jnp.minimum(jnp.maximum(x, jnp.maximum(0, c2[d] - limit)), jnp.minimum(limit, c2[d]))

    a = [clamp(d, lax.shift_right_arithmetic(c2[d] + c3[d] - c1[d] + 1, 1)) for d in range(4)]
    for d in range(4):
        b = [c2[e] - a[e] for e in range(4)]

        def down(s):
            return a[(s - 2) % 4] + c1[(s - 1) % 4] + a[(s - 1) % 4]

        def up(s):
            return b[(s + 2) % 4] + c3[(s + 1) % 4] + b[(s + 1) % 4]

        m = jnp.maximum(down((d + 2) % 4), down((d + 1) % 4)) - a[d]
        n = jnp.maximum(up((d + 2) % 4), up((d + 3) % 4)) - b[d]
        a[d] = clamp(d, lax.shift_right_arithmetic(n + c2[d] - m + 1, 1))
    top = jnp.int32(0)
    for s in range(4):
        d1, d2, u1 = (s - 1) % 4, (s - 2) % 4, (s + 1) % 4
        below = jnp.maximum(free, a[d2] + c1[d1]) + a[d1]
        above = jnp.maximum(free, c2[d2] - a[d2] + c3[u1]) + c2[u1] - a[u1]
        top = jnp.maximum(top, jnp.maximum(below, above))
        top = jnp.where(c2[s] > 2 * limit, CAPACITY, top)
    narrow = top <= LEVELS[-2][0]
    a = [jnp.where(narrow, a[d], lax.shift_right_logical(c2[d] + 1, 1)) for d in range(4)]
    opened = jnp.where(narrow, free, WIDE[2])
    level = jnp.int32(0)
    for size, _, _ in LEVELS[:-1]:
        level = level + jnp.where(top > size, 1, 0)
    level_ref[0] = level
    b = [c2[d] - a[d] for d in range(4)]

    def at(values, index):
        index = lax.rem(index + 8, 4)
        out = values[3]
        for i in range(3):
            out = jnp.where(index == i, values[i], out)
        return out

    def entry(row, i):
        v = lists[row + i]
        return jnp.minimum(jnp.maximum(v, 0), CHIP - 1)

    d1, d2, u1 = lax.rem(chip + 3, 4), lax.rem(chip + 2, 4), lax.rem(chip + 1, 4)
    far_row = (d2 * 4 + 2) * 32
    a_far, b_far = at(a, d2), at(b, d2)
    down_fwd = jnp.maximum(opened, a_far + at(c1, d1))
    up_fwd = jnp.maximum(opened, b_far + at(c3, u1))
    for i in range(CAPACITY):
        plan_ref[i] = 0
        plan_ref[CAPACITY + i] = 0
    for i in range(WIDE[1]):
        plan_ref[i] = entry(far_row, i)
        plan_ref[CAPACITY + i] = entry(far_row, a_far + i)
    for i in range(PART):
        plan_ref[a_far + i] = entry((d1 * 4 + 1) * 32, i)
        plan_ref[CAPACITY + b_far + i] = entry((u1 * 4 + 3) * 32, i)
    for i in range(WIDE[1]):
        plan_ref[down_fwd + i] = CHIP + i
        plan_ref[CAPACITY + up_fwd + i] = CHIP + i

    own_a = at(a, chip)
    from_up = at(a, chip + 3)
    from_down = at(b, chip + 1)
    far_down = jnp.maximum(opened, at(a, chip + 3) + at(c1, chip))
    far_up = jnp.maximum(opened, at(b, chip + 1) + at(c3, chip))
    for j in range(PART):
        old = anc_ref[member * PART + j]
        src = third(old)
        k = lax.rem(src - chip + 4, 4)
        r = ranks[chip * 96 + old]
        far = jnp.where(r < own_a, CHIP + far_down + r, CHIP + CAPACITY + far_up + r - own_a)
        where = jnp.where(
            k == 0,
            old - src * CHIP,
            jnp.where(
                k == 1,
                CHIP + from_up + r,
                jnp.where(k == 3, CHIP + CAPACITY + from_down + r, far),
            ),
        )
        plan_ref[GATHER_AT + j] = where


def make_plan(ancestors):
    return pl.pallas_call(
        plan_kernel,
        out_shape=(jax.ShapeDtypeStruct((64,), jnp.int32), jax.ShapeDtypeStruct((1,), jnp.int32)),
        in_specs=[pl.BlockSpec(memory_space=pltpu.SMEM)],
        out_specs=(pl.BlockSpec(memory_space=pltpu.SMEM), pl.BlockSpec(memory_space=pltpu.SMEM)),
        scratch_shapes=[
            pltpu.SMEM((4 * 96,), jnp.int32),
            pltpu.SMEM((4 * 96,), jnp.int32),
            pltpu.SMEM((16 * 32,), jnp.int32),
        ],
    )(ancestors)


def one_step(u_at, v_at, h_at, h_rows, v_rows, put_u, put_v, put_h, cor, obs, nud, force, tiles):
    blocks = LAT // 8
    lane = lax.broadcasted_iota(jnp.int32, (8, 128), 1)
    lane_first, lane_last = lane == 0, lane == 127

    def across(q):
        after = [pltpu.roll(x, 127, 1) for x in q]
        before = [pltpu.roll(x, 1, 1) for x in q]
        if tiles == 1:
            return [after[0] - before[0]]
        return [
            jnp.where(lane_last, after[1], after[0]) - before[0],
            after[1] - jnp.where(lane_first, before[0], before[1]),
        ]

    def along(ref, r, t):
        return ref[t, pl.ds(8 * r + 9, 8), :] - ref[t, pl.ds(8 * r + 7, 8), :]

    dxu, centre = [], []

    def finish(r):
        for t in range(tiles):
            x = centre[r][t]
            put_h(
                r, t,
                x - 0.125 * (dxu[r][t] + along(v_rows, r, t)) + nud(r, t) * (obs(r, t) - x) + force(r, t),
            )

    for r in range(blocks):
        h = [h_at(r, t) for t in range(tiles)]
        centre.append(h)
        dxh = across(h)
        f = cor(r)
        u_new = []
        for t in range(tiles):
            u, v = u_at(r, t), v_at(r, t)
            u_new.append(u + f * v - 0.125 * dxh[t])
            v_new = v - f * u - 0.125 * along(h_rows, r, t)
            put_u(r, t, u_new[t])
            put_v(r, t, v_new)
            v_rows[t, 8 * r + 8:8 * r + 16, :] = v_new
        dxu.append(across(u_new))
        if r:
            finish(r - 1)
    finish(blocks - 1)


def block(ref, lead, r, t):
    return ref[(*lead, slice(8 * r, 8 * r + 8), slice(128 * t, 128 * t + 128))]


def put(ref, lead, r, t, x):
    ref[(*lead, slice(8 * r, 8 * r + 8), slice(128 * t, 128 * t + 128))] = x


def three_steps(start, result, hs, vs, us, cor_v, obs, nud, force, tiles):
    for r in range(LAT // 8):
        for t in range(tiles):
            hs[0, t, 8 * r + 8:8 * r + 16, :] = start(2, r, t)
    for step in range(STEPS):
        now, later, last = step % 2, (step + 1) % 2, step == STEPS - 1

        def padded(ref, at):
            return lambda r, t: ref[at, t, 8 * r + 8:8 * r + 16, :]

        def store(f, ref):
            def go(r, t, x):
                if last:
                    result(f, r, t, x)
                elif f != 1:
                    ref[later, t, 8 * r + 8:8 * r + 16, :] = x
            return go

        one_step(
            (lambda r, t: start(0, r, t)) if step == 0 else padded(us, now),
            (lambda r, t: start(1, r, t)) if step == 0 else padded(vs, now),
            padded(hs, now), hs.at[now], vs.at[later],
            store(0, us), store(1, vs), store(2, hs),
            lambda r: block(cor_v, (), r, 0), obs, nud, functools.partial(force, step), tiles,
        )


def cycle_kernel(
    level, plan, ens_hbm, pert_hbm, obs_hbm, prec_hbm, nud_hbm,
    slots, lw_out,
    ens, pert, fields, cor_v, pool, first, stage, msg_out, msg_in, edges, win, half, edge, hs, vs, us,
    misfit, zbuf, xbuf, lwbuf,
    in_sem, const_sem, halo_send, halo_recv, pool_send, pool_recv,
    edge_sem, ring_send, ring_recv, mir_send, mir_recv, out_sem,
    z_send, z_recv, x_send, x_recv, m_send, m_recv,
):
    size, far, opened = level
    member, lon = lax.axis_index("member"), lax.axis_index("lon")
    core = lax.rem(member, 2)
    lon_x, lon_z = lax.div(lon, 4), lax.rem(lon, 4)
    sibling = {"member": member + 1 - 2 * core}
    ring = ({"member": lax.rem(member + 6, 8)}, {"member": lax.rem(member + 2, 8)})
    sides = ({"lon": lax.rem(lon + 15, 16)}, {"lon": lax.rem(lon + 1, 16)})
    z_peers = [{"lon": lon_x * 4 + lax.rem(lon_z + k, 4)} for k in range(1, 4)]
    x_peers = [{"lon": lax.rem(lon_x + k, 4) * 4 + lon_z} for k in range(1, 4)]
    m_peers = [{"member": lax.rem(member + k, 8)} for k in range(1, 8)]

    def remote(src, dst, ssem, rsem, to):
        return pltpu.make_async_remote_copy(
            src_ref=src, dst_ref=dst, send_sem=ssem, recv_sem=rsem, device_id=to, device_id_type=MESH
        )

    loads = []
    for g in range(3):
        part = pl.ds(4 * g, 4)
        loads.append((
            pltpu.make_async_copy(ens_hbm.at[part], ens.at[part], in_sem.at[0, g]),
            pltpu.make_async_copy(pert_hbm.at[part], pert.at[part], in_sem.at[1, g]),
        ))
    consts = [
        pltpu.make_async_copy(ref, fields.at[i], const_sem.at[i])
        for i, ref in enumerate((obs_hbm, prec_hbm, nud_hbm))
    ]
    for cp in consts:
        cp.start()
    for pair in loads:
        for cp in pair:
            cp.start()

    barrier = pltpu.get_barrier_semaphore()
    everyone = list(sides) + z_peers + x_peers + m_peers
    for peer in everyone:
        pl.semaphore_signal(barrier, inc=1, device_id=peer, device_id_type=MESH)

    row_at = lax.broadcasted_iota(jnp.int32, (LAT, 128), 0).astype(F32)
    cor_v[...] = 0.3 * jnp.sin(math.pi * (row_at + 0.5 - LAT / 2) / LAT)

    for ref in (hs, vs):
        for n in range(2):
            for t in range(2):
                ref[n, t, 0:8, :] = jnp.zeros((8, 128), F32)
                ref[n, t, LAT + 8:LAT + 16, :] = jnp.zeros((8, 128), F32)

    for cp in consts:
        cp.wait()

    lane = lax.broadcasted_iota(jnp.int32, (LAT, 128), 1)

    def tile(which, p, side):
        cut = slice(0, 128) if side == 0 else slice(128, 256)
        if which < 3:
            return ens[p, which, :, cut]
        if which < 6:
            return pert[p, which - 3, :, cut]
        return fields[0 if which == 6 else 2, :, cut]

    def turned(x, by):
        by = by % 128
        return x if by == 0 else pltpu.roll(x, by, 1)

    within = lane & (STRIDE - 1)

    def outer(which, p, q):
        return turned(jnp.where(lane < 64, tile(which, p, 0), tile(which, p, 1)), STRIDE * q + HALO)

    def spot(which, group):
        return which, (group if which < 6 else 0)

    for group in range(TILES):
        for cp in loads[group]:
            cp.wait()
        for which in range(8 if group == 0 else 6):
            start = acc = outer(which, group * GROUP, 0)
            for q in range(1, GROUP):
                acc = jnp.where(lane >= STRIDE * q - HALO, outer(which, group * GROUP + q, q), acc)
            edges[which, group] = jnp.where(lane >= 128 - HALO, start, acc)

        for side in range(2):
            acc = None
            for which, width, to in PIECES:
                source = HALO if side == 0 else HALO - width
                x = turned(edges[spot(which, group)], to - source)
                acc = x if acc is None else jnp.where(within >= to, x, acc)
            msg_out[side, group] = acc

    pl.semaphore_wait(barrier, len(everyone))
    halos = [
        remote(msg_out.at[s], msg_in.at[1 - s], halo_send.at[s], halo_recv.at[1 - s], sides[s])
        for s in range(2)
    ]
    for cp in halos:
        cp.start()

    def share(on_core, group):
        part = pool.at[pl.ds(on_core * PART + GROUP * group, GROUP)]
        return remote(part, part, pool_send.at[group], pool_recv.at[group], sibling)

    def interior(p, carry):
        at = core * PART + p
        three_steps(
            lambda f, r, t: block(ens, (p, f), r, t), lambda f, r, t, x: put(pool, (at, f), r, t, x),
            hs, vs, us, cor_v, lambda r, t: block(fields, (0,), r, t), lambda r, t: block(fields, (2,), r, t),
            lambda step, r, t: block(pert, (p, step), r, t), 2,
        )
        return carry

    def interiors(group, carry):
        lax.fori_loop(GROUP * group, GROUP * group + GROUP, interior, 0)
        share(core, group).start()
        return carry

    lax.fori_loop(0, TILES, interiors, 0)

    for s in range(2):
        remote(msg_out.at[s], msg_in.at[s], halo_send.at[s], halo_recv.at[s], sides[s]).wait_recv()

    def edge_copy(on_core, group):
        part = edge.at[on_core, group]
        return remote(part, part, edge_sem.at[0, group], edge_sem.at[1, group], sibling)

    def edge_group(n, carry):
        for s in range(2):
            for which, width, at in PIECES:
                to = HALO - width if s == 0 else HALO
                x = turned(msg_in[s, n], to - at)
                inside = (within >= to) & (within < to + width)
                win[s, which, n] = jnp.where(inside, x, edges[which, n if which < 6 else 0])
            win[s, 5, n] = edges[5, n]
            three_steps(
                lambda f, r, t: block(win, (s, f, n), r, t), lambda f, r, t, x: put(half, (s, f), r, t, x),
                hs, vs, us, cor_v, lambda r, t: block(win, (s, 6, n), r, t),
                lambda r, t: block(win, (s, 7, n), r, t), lambda step, r, t: block(win, (s, 3 + step, n), r, t), 1,
            )
        for f in range(3):
            edge[core, n, f] = jnp.where((within >= HALO) & (within < 2 * HALO), half[0, f], half[1, f])
        edge_copy(core, n).start()
        return carry

    lax.fori_loop(0, TILES, edge_group, 0)
    for group in range(TILES):
        share(1 - core, group).wait_recv()
    for group in range(TILES):
        edge_copy(1 - core, group).wait_recv()

    def whole(i):
        on = jnp.where(i >= PART, 1, 0)
        p = i - on * PART
        group = lax.shift_right_logical(p, 2)
        back = 128 - HALO - STRIDE * (p - GROUP * group)
        out = []
        for f in range(3):
            x = pltpu.roll(edge[on, group, f], back, 1)
            low = jnp.where(lane < HALO, x, pool[i, f, :, 0:128])
            high = jnp.where(lane >= 128 - HALO, x, pool[i, f, :, 128:256])
            out.append((low, high))
        return out

    positions = (size + 1) // 2
    open_pos, far_pos = opened // 2, far // 2

    def split(pos):
        return 2 * pos + 1 == size

    def entry_at(pos, on_core):
        return 2 * pos if split(pos) else 2 * pos + on_core

    def rows(ref, pos, on_core):
        return ref.at[:, pl.ds(on_core * (LAT // 2), LAT // 2), :] if split(pos) else ref

    def landing(way, pos, on_core):
        i = entry_at(pos, on_core)
        if pos < far_pos:
            return first.at[way, i]
        return rows(slots.at[CHIP + way * CAPACITY + i], pos, on_core)

    def ring_copy(way, pos):
        return remote(
            rows(stage.at[way, pos], pos, core), landing(way, pos, core),
            ring_send.at[way, pos], ring_recv.at[way, pos], ring[way],
        )

    def mirror_copy(way, pos, on_core):
        ref = landing(way, pos, on_core)
        return remote(ref, ref, mir_send.at[way, pos], mir_recv.at[way, pos], sibling)

    for pos in range(open_pos):
        for way in range(2):
            parts = whole(plan[way * CAPACITY + entry_at(pos, core)])
            for f in range(3):
                stage[way, pos, f, :, 0:128], stage[way, pos, f, :, 128:256] = parts[f]
            ring_copy(way, pos).start()

    for group in range(TILES):
        share(core, group).wait_send()

    def complete(i, carry):
        parts = whole(i)
        for f in range(3):
            pool[i, f, :, 0:128], pool[i, f, :, 128:256] = parts[f]
        lo = fields[0, :, 0:128] - parts[2][0]
        hi = fields[0, :, 128:256] - parts[2][1]
        term = fields[1, :, 0:128] * lo * lo + fields[1, :, 128:256] * hi * hi
        misfit[i] = jnp.sum(term.reshape(LAT // 8, 8, 128), axis=0)
        return carry

    lax.fori_loop(0, CHIP, complete, 0)
    keep = [pltpu.make_async_copy(pool, slots.at[pl.ds(0, CHIP)], out_sem.at[0])]
    keep[0].start()

    total = jnp.sum(jnp.sum(misfit[pl.ds(core * PART, PART)], axis=1), axis=1, keepdims=True)
    small = lax.broadcasted_iota(jnp.int32, (PART, 128), 1)
    which = lax.broadcasted_iota(jnp.int32, (PART, 128), 0)
    line = jnp.sum(jnp.where(small == which, total, 0.0), axis=0, keepdims=True)
    zbuf[lon_z] = jnp.broadcast_to(line, (8, 128))
    z_copies = [
        remote(zbuf.at[lon_z], zbuf.at[lon_z], z_send.at[k], z_recv.at[k], z_peers[k]) for k in range(3)
    ]
    for cp in z_copies:
        cp.start()

    for k in range(3):
        z_copies[k].wait_send()
        z_copies[k].wait_recv()
    xbuf[lon_x] = ((zbuf[0] + zbuf[1]) + zbuf[2]) + zbuf[3]
    x_copies = [
        remote(xbuf.at[lon_x], xbuf.at[lon_x], x_send.at[k], x_recv.at[k], x_peers[k]) for k in range(3)
    ]
    for cp in x_copies:
        cp.start()
    for cp in x_copies:
        cp.wait_send()
        cp.wait_recv()
    lwbuf[member] = ((xbuf[0] + xbuf[1]) + xbuf[2]) + xbuf[3]
    m_copies = [
        remote(lwbuf.at[member], lwbuf.at[member], m_send.at[k], m_recv.at[k], m_peers[k]) for k in range(7)
    ]
    for cp in m_copies:
        cp.start()

    for pos in range(far_pos):
        for way in range(2):
            ring_copy(way, pos).wait_recv()
            mirror_copy(way, pos, core).start()
    for pos in range(far_pos):
        for way in range(2):
            mirror_copy(way, pos, 1 - core).wait_recv()
    for way in range(2):
        cp = pltpu.make_async_copy(
            first.at[way], slots.at[pl.ds(CHIP + way * CAPACITY, far)], out_sem.at[1 + way]
        )
        cp.start()
        keep.append(cp)
    for pos in range(open_pos, positions):
        for way in range(2):
            idx = plan[way * CAPACITY + entry_at(pos, core)]
            own = pool[jnp.minimum(idx, CHIP - 1)]
            passed = first[way, jnp.clip(idx - CHIP, 0, far - 1)]
            stage[way, pos] = jnp.where(idx < CHIP, own, passed)
            ring_copy(way, pos).start()
    for pos in range(far_pos, positions):
        for way in range(2):
            ring_copy(way, pos).wait_recv()
            mirror_copy(way, pos, core).start()

    for cp in m_copies:
        cp.wait_send()
        cp.wait_recv()
    lw_out[...] = lwbuf[...]
    for cp in halos:
        cp.wait_send()
    for group in range(TILES):
        edge_copy(core, group).wait_send()
    for pos in range(positions):
        for way in range(2):
            ring_copy(way, pos).wait_send()
    for pos in range(positions):
        for way in range(2):
            mirror_copy(way, pos, core).wait_send()
            if pos >= far_pos:
                mirror_copy(way, pos, 1 - core).wait_recv()
    for cp in keep:
        cp.wait()


def run_cycle(level, number, plan, ensemble, perturbation, observed, precision, nudging):
    anywhere = pl.BlockSpec(memory_space=pltpu.HBM)
    dma = pltpu.SemaphoreType.DMA
    most = (level[0] + 1) // 2
    return pl.pallas_call(
        functools.partial(cycle_kernel, level),
        out_shape=(
            jax.ShapeDtypeStruct((SLOTS, 3, LAT, CLON), F32),
            jax.ShapeDtypeStruct((8, 8, 128), F32),
        ),
        in_specs=[pl.BlockSpec(memory_space=pltpu.SMEM)] + [anywhere] * 5,
        out_specs=(anywhere, pl.BlockSpec(memory_space=pltpu.VMEM)),
        scratch_shapes=[
            pltpu.VMEM((PART, 3, LAT, CLON), F32),
            pltpu.VMEM((PART, 3, LAT, CLON), F32),
            pltpu.VMEM((3, LAT, CLON), F32),
            pltpu.VMEM((LAT, 128), F32),
            pltpu.VMEM((CHIP, 3, LAT, CLON), F32),
            pltpu.VMEM((2, level[1], 3, LAT, CLON), F32),
            pltpu.VMEM((2, most, 3, LAT, CLON), F32),
            pltpu.VMEM((2, 3, LAT, 128), F32),
            pltpu.VMEM((2, 3, LAT, 128), F32),
            pltpu.VMEM((8, TILES, LAT, 128), F32),
            pltpu.VMEM((2, 8, TILES, LAT, 128), F32),
            pltpu.VMEM((2, 3, LAT, 128), F32),
            pltpu.VMEM((2, TILES, 3, LAT, 128), F32),
            pltpu.VMEM((2, 2, LAT + 16, 128), F32),
            pltpu.VMEM((2, 2, LAT + 16, 128), F32),
            pltpu.VMEM((2, 2, LAT + 16, 128), F32),
            pltpu.VMEM((CHIP, 8, 128), F32),
            pltpu.VMEM((4, 8, 128), F32),
            pltpu.VMEM((4, 8, 128), F32),
            pltpu.VMEM((8, 8, 128), F32),
            dma((2, 3)), dma((3,)), dma((2,)), dma((2,)), dma((TILES,)), dma((TILES,)), dma((2, TILES)),
            dma((2, most)), dma((2, most)), dma((2, most)), dma((2, most)), dma((3,)),
            dma((3,)), dma((3,)), dma((3,)), dma((3,)), dma((7,)), dma((7,)),
        ],
        compiler_params=pltpu.CompilerParams(
            collective_id=number, has_side_effects=True, vmem_limit_bytes=50 * 2**20
        ),
    )(plan, ensemble, perturbation, observed, precision, nudging)


def resample_kernel(plan, lw_ref, slots, weights_ref, analysis, held, in_sem, out_sem):
    ins = [
        pltpu.make_async_copy(slots.at[plan[GATHER_AT + j]], held.at[j], in_sem.at[j]) for j in range(PART)
    ]
    outs = [pltpu.make_async_copy(held.at[j], analysis.at[j], out_sem.at[j]) for j in range(PART)]
    for cp in ins:
        cp.start()
    lane = lax.broadcasted_iota(jnp.int32, (8, 8, 128), 2)
    logw = jnp.where(lane < PART, lw_ref[...] * (-2.0 / (LAT * CLON * 16)), -jnp.inf)
    top = jnp.max(jnp.max(logw, axis=0), axis=1, keepdims=True)
    e = jnp.exp(logw - top[None])
    whole = jnp.sum(jnp.sum(e, axis=0), axis=1, keepdims=True)
    own = jnp.where(
        lax.broadcasted_iota(jnp.int32, (8, 8, 128), 0) == lax.axis_index("member"), e, 0.0
    )
    row = jnp.sum(own, axis=0) / whole
    weights_ref[...] = row[0, :PART]
    for j in range(PART):
        ins[j].wait()
        outs[j].start()
    for cp in outs:
        cp.wait()


def resample(plan, lw, slots):
    return pl.pallas_call(
        resample_kernel,
        out_shape=(
            jax.ShapeDtypeStruct((PART,), F32),
            jax.ShapeDtypeStruct((PART, 3, LAT, CLON), F32),
        ),
        in_specs=[
            pl.BlockSpec(memory_space=pltpu.SMEM),
            pl.BlockSpec(memory_space=pltpu.VMEM),
            pl.BlockSpec(memory_space=pltpu.HBM),
        ],
        out_specs=(pl.BlockSpec(memory_space=pltpu.VMEM), pl.BlockSpec(memory_space=pltpu.HBM)),
        scratch_shapes=[
            pltpu.VMEM((PART, 3, LAT, CLON), F32),
            pltpu.SemaphoreType.DMA((PART,)),
            pltpu.SemaphoreType.DMA((PART,)),
        ],
    )(plan, lw, slots)


def body(ensemble, perturbation, observed, precision, nudging, ancestors):
    plan, level = make_plan(ancestors)
    operands = (plan, ensemble, perturbation, observed, precision, nudging)
    branches = [functools.partial(run_cycle, form, n) for n, form in enumerate(LEVELS)]
    if len(branches) == 1:
        slots, lw = branches[0](*operands)
    else:
        slots, lw = lax.switch(level.reshape(()), branches, *operands)
    weights, analysis = resample(plan, lw, slots)
    return weights, analysis


def solution(mesh):
    placed = (
        P("member", None, None, "lon"),
        P("member", None, None, "lon"),
        P(None, "lon"),
        P(None, "lon"),
        P(None, "lon"),
        P(),
    )
    return jax.shard_map(
        body,
        mesh=mesh,
        in_specs=placed,
        out_specs=(P("member"), P("member", None, None, "lon")),
        check_vma=False,
    )
```

```python
import functools
import math

import jax
import jax.numpy as jnp
from jax import lax
from jax.experimental import pallas as pl
from jax.experimental.pallas import tpu as pltpu
from jax.sharding import PartitionSpec as P

MESH = pl.DeviceIdType.MESH
F32 = jnp.float32
STEPS = 3
LAT = 64
CLON = 256
PART = 12
CHIP = 24
HALO = 6
STRIDE = 32
GROUP = 4
TILES = PART // GROUP
PIECES = ((2, 6, 0), (0, 5, 6), (1, 5, 11), (3, 4, 16), (4, 2, 20), (6, 4, 22), (7, 4, 26))
CAPACITY = 24
NARROW = (4, 6)
WIDE = (6, 8)
LEVELS = ((11, *NARROW), (12, *NARROW), (13, *NARROW), (14, *WIDE), (16, *WIDE), (CAPACITY, *WIDE))
SLOTS = CHIP + 2 * CAPACITY
GATHER_AT = 2 * CAPACITY


def plan_kernel(anc_ref, plan_ref, level_ref, need, ranks, lists):
    member = lax.axis_index("member")
    chip = lax.div(member, 2)

    def third(a):
        return lax.shift_right_logical(a * 2731, 16)

    for i in range(4 * 96):
        need[i] = 0
    for j in range(96):
        need[(j // CHIP) * 96 + anc_ref[j]] = 1
    counts = {}
    for d in range(4):
        for k in range(1, 4):
            first = d * 96 + (d + k) % 4 * CHIP
            counts[d, k] = sum((need[first + p] for p in range(1, CHIP)), need[first])
    for k in range(1, 4):
        src = lax.rem(chip + k, 4)
        dst = lax.rem(chip + 4 - k, 4)
        rank, cnt = jnp.int32(0), jnp.int32(0)
        for p in range(CHIP):
            ranks[src * CHIP + p] = rank
            rank = rank + need[chip * 96 + src * CHIP + p]
            lists[k * 32 + cnt] = p
            cnt = cnt + need[dst * 96 + chip * CHIP + p]
    c1 = [counts[d, 1] for d in range(4)]
    c2 = [counts[d, 2] for d in range(4)]
    c3 = [counts[d, 3] for d in range(4)]

    def balance(limit, free):
        def clamp(d, x):
            return jnp.minimum(jnp.maximum(x, jnp.maximum(0, c2[d] - limit)), jnp.minimum(limit, c2[d]))

        a = [clamp(d, lax.shift_right_arithmetic(c2[d] + c3[d] - c1[d] + 1, 1)) for d in range(4)]
        for d in range(4):
            b = [c2[e] - a[e] for e in range(4)]

            def down(s):
                return a[(s - 2) % 4] + c1[(s - 1) % 4] + a[(s - 1) % 4]

            def up(s):
                return b[(s + 2) % 4] + c3[(s + 1) % 4] + b[(s + 1) % 4]

            m = jnp.maximum(down((d + 2) % 4), down((d + 1) % 4)) - a[d]
            n = jnp.maximum(up((d + 2) % 4), up((d + 3) % 4)) - b[d]
            a[d] = clamp(d, lax.shift_right_arithmetic(n + c2[d] - m + 1, 1))
        top = jnp.int32(0)
        for s in range(4):
            d1, d2, u1 = (s - 1) % 4, (s - 2) % 4, (s + 1) % 4
            below = jnp.maximum(free, a[d2] + c1[d1]) + a[d1]
            above = jnp.maximum(free, c2[d2] - a[d2] + c3[u1]) + c2[u1] - a[u1]
            top = jnp.maximum(top, jnp.maximum(below, above))
            top = jnp.where(c2[s] > 2 * limit, CAPACITY, top)
        return a, top

    tight, tight_top = balance(*NARROW)
    loose, loose_top = balance(*WIDE)
    narrow = tight_top <= LEVELS[2][0]
    fits = loose_top <= LEVELS[4][0]
    a = [
        jnp.where(narrow, tight[d], jnp.where(fits, loose[d], lax.shift_right_logical(c2[d] + 1, 1)))
        for d in range(4)
    ]
    opened = jnp.where(narrow, NARROW[1], WIDE[1])
    level = jnp.where(tight_top > LEVELS[0][0], 1, 0) + jnp.where(tight_top > LEVELS[1][0], 1, 0)
    other = 3 + jnp.where(loose_top > LEVELS[3][0], 1, 0) + jnp.where(loose_top > LEVELS[4][0], 1, 0)
    level_ref[0] = jnp.where(narrow, level, other)
    b = [c2[d] - a[d] for d in range(4)]

    def at(values, index):
        index = lax.rem(index + 8, 4)
        out = values[3]
        for i in range(3):
            out = jnp.where(index == i, values[i], out)
        return out

    def entry(row, i):
        v = lists[row + i]
        return jnp.minimum(jnp.maximum(v, 0), CHIP - 1)

    d1, d2, u1 = lax.rem(chip + 3, 4), lax.rem(chip + 2, 4), lax.rem(chip + 1, 4)
    far_row = 2 * 32
    a_far, b_far = at(a, d2), at(b, d2)
    down_fwd = jnp.maximum(opened, a_far + at(c1, d1))
    up_fwd = jnp.maximum(opened, b_far + at(c3, u1))
    for i in range(CAPACITY):
        plan_ref[i] = 0
        plan_ref[CAPACITY + i] = 0
    for i in range(WIDE[0]):
        plan_ref[i] = entry(far_row, i)
        plan_ref[CAPACITY + i] = entry(far_row, a_far + i)
    for i in range(PART):
        plan_ref[a_far + i] = entry(1 * 32, i)
        plan_ref[CAPACITY + b_far + i] = entry(3 * 32, i)
    for i in range(WIDE[0]):
        plan_ref[down_fwd + i] = CHIP + i
        plan_ref[CAPACITY + up_fwd + i] = CHIP + i

    own_a = at(a, chip)
    from_up = at(a, chip + 3)
    from_down = at(b, chip + 1)
    far_down = jnp.maximum(opened, at(a, chip + 3) + at(c1, chip))
    far_up = jnp.maximum(opened, at(b, chip + 1) + at(c3, chip))
    for j in range(PART):
        old = anc_ref[member * PART + j]
        src = third(old)
        k = lax.rem(src - chip + 4, 4)
        r = ranks[old]
        far = jnp.where(r < own_a, CHIP + far_down + r, CHIP + CAPACITY + far_up + r - own_a)
        where = jnp.where(
            k == 0,
            old - src * CHIP,
            jnp.where(
                k == 1,
                CHIP + from_up + r,
                jnp.where(k == 3, CHIP + CAPACITY + from_down + r, far),
            ),
        )
        plan_ref[GATHER_AT + j] = where


def make_plan(ancestors):
    return pl.pallas_call(
        plan_kernel,
        out_shape=(jax.ShapeDtypeStruct((64,), jnp.int32), jax.ShapeDtypeStruct((1,), jnp.int32)),
        in_specs=[pl.BlockSpec(memory_space=pltpu.SMEM)],
        out_specs=(pl.BlockSpec(memory_space=pltpu.SMEM), pl.BlockSpec(memory_space=pltpu.SMEM)),
        scratch_shapes=[
            pltpu.SMEM((4 * 96,), jnp.int32),
            pltpu.SMEM((96,), jnp.int32),
            pltpu.SMEM((4 * 32,), jnp.int32),
        ],
    )(ancestors)


def one_step(u_at, v_at, h_at, h_rows, v_rows, put_u, put_v, put_h, cor, obs, nud, force, tiles):
    blocks = LAT // 8
    lane = lax.broadcasted_iota(jnp.int32, (8, 128), 1)
    lane_first, lane_last = lane == 0, lane == 127

    def across(q):
        after = [pltpu.roll(x, 127, 1) for x in q]
        before = [pltpu.roll(x, 1, 1) for x in q]
        if tiles == 1:
            return [after[0] - before[0]]
        return [
            jnp.where(lane_last, after[1], after[0]) - before[0],
            after[1] - jnp.where(lane_first, before[0], before[1]),
        ]

    def along(ref, r, t):
        return ref[t, pl.ds(8 * r + 9, 8), :] - ref[t, pl.ds(8 * r + 7, 8), :]

    dxu, centre = [], []

    def finish(r):
        for t in range(tiles):
            x = centre[r][t]
            put_h(
                r, t,
                x - 0.125 * (dxu[r][t] + along(v_rows, r, t)) + nud(r, t) * (obs(r, t) - x) + force(r, t),
            )

    for r in range(blocks):
        h = [h_at(r, t) for t in range(tiles)]
        centre.append(h)
        dxh = across(h)
        f = cor(r)
        u_new = []
        for t in range(tiles):
            u, v = u_at(r, t), v_at(r, t)
            u_new.append(u + f * v - 0.125 * dxh[t])
            v_new = v - f * u - 0.125 * along(h_rows, r, t)
            put_u(r, t, u_new[t])
            put_v(r, t, v_new)
            v_rows[t, 8 * r + 8:8 * r + 16, :] = v_new
        dxu.append(across(u_new))
        if r:
            finish(r - 1)
    finish(blocks - 1)


def block(ref, lead, r, t):
    return ref[(*lead, slice(8 * r, 8 * r + 8), slice(128 * t, 128 * t + 128))]


def put(ref, lead, r, t, x):
    ref[(*lead, slice(8 * r, 8 * r + 8), slice(128 * t, 128 * t + 128))] = x


def three_steps(start, result, hs, vs, us, cor_v, obs, nud, force, tiles):
    for r in range(LAT // 8):
        for t in range(tiles):
            hs[0, t, 8 * r + 8:8 * r + 16, :] = start(2, r, t)
    for step in range(STEPS):
        now, later, last = step % 2, (step + 1) % 2, step == STEPS - 1

        def padded(ref, at):
            return lambda r, t: ref[at, t, 8 * r + 8:8 * r + 16, :]

        def store(f, ref):
            def go(r, t, x):
                if last:
                    result(f, r, t, x)
                elif f != 1:
                    ref[later, t, 8 * r + 8:8 * r + 16, :] = x
            return go

        one_step(
            (lambda r, t: start(0, r, t)) if step == 0 else padded(us, now),
            (lambda r, t: start(1, r, t)) if step == 0 else padded(vs, now),
            padded(hs, now), hs.at[now], vs.at[later],
            store(0, us), store(1, vs), store(2, hs),
            lambda r: block(cor_v, (), r, 0), obs, nud, functools.partial(force, step), tiles,
        )


def cycle_kernel(
    level, plan, ens_hbm, pert_hbm, obs_hbm, prec_hbm, nud_hbm,
    slots, lw_out,
    ens, pert, fields, cor_v, pool, first, stage, msg_out, msg_in, edges, win, half, edge, hs, vs, us,
    misfit, zbuf, xbuf, lwbuf,
    in_sem, const_sem, halo_send, halo_recv, pool_send, pool_recv,
    edge_sem, ring_send, ring_recv, mir_send, mir_recv, out_sem,
    z_send, z_recv, x_send, x_recv, m_send, m_recv,
):
    size, far, opened = level
    member, lon = lax.axis_index("member"), lax.axis_index("lon")
    core = lax.rem(member, 2)
    lon_x, lon_z = lax.div(lon, 4), lax.rem(lon, 4)
    sibling = {"member": member + 1 - 2 * core}
    ring = ({"member": lax.rem(member + 6, 8)}, {"member": lax.rem(member + 2, 8)})
    sides = ({"lon": lax.rem(lon + 15, 16)}, {"lon": lax.rem(lon + 1, 16)})
    z_peers = [{"lon": lon_x * 4 + lax.rem(lon_z + k, 4)} for k in range(1, 4)]
    x_peers = [{"lon": lax.rem(lon_x + k, 4) * 4 + lon_z} for k in range(1, 4)]
    m_peers = [{"member": lax.rem(member + k, 8)} for k in range(1, 8)]

    def remote(src, dst, ssem, rsem, to):
        return pltpu.make_async_remote_copy(
            src_ref=src, dst_ref=dst, send_sem=ssem, recv_sem=rsem, device_id=to, device_id_type=MESH
        )

    loads = []
    for g in range(3):
        part = pl.ds(4 * g, 4)
        loads.append((
            pltpu.make_async_copy(ens_hbm.at[part], ens.at[part], in_sem.at[0, g]),
            pltpu.make_async_copy(pert_hbm.at[part], pert.at[part], in_sem.at[1, g]),
        ))
    consts = [
        pltpu.make_async_copy(ref, fields.at[i], const_sem.at[i])
        for i, ref in enumerate((obs_hbm, prec_hbm, nud_hbm))
    ]
    for cp in consts:
        cp.start()
    for pair in loads:
        for cp in pair:
            cp.start()

    barrier = pltpu.get_barrier_semaphore()
    everyone = list(sides) + z_peers + x_peers + m_peers
    for peer in everyone:
        pl.semaphore_signal(barrier, inc=1, device_id=peer, device_id_type=MESH)

    row_at = lax.broadcasted_iota(jnp.int32, (LAT, 128), 0).astype(F32)
    cor_v[...] = 0.3 * jnp.sin(math.pi * (row_at + 0.5 - LAT / 2) / LAT)

    for ref in (hs, vs):
        for n in range(2):
            for t in range(2):
                ref[n, t, 0:8, :] = jnp.zeros((8, 128), F32)
                ref[n, t, LAT + 8:LAT + 16, :] = jnp.zeros((8, 128), F32)

    for cp in consts:
        cp.wait()

    lane = lax.broadcasted_iota(jnp.int32, (LAT, 128), 1)

    def tile(which, p, side):
        cut = slice(0, 128) if side == 0 else slice(128, 256)
        if which < 3:
            return ens[p, which, :, cut]
        if which < 6:
            return pert[p, which - 3, :, cut]
        return fields[0 if which == 6 else 2, :, cut]

    def turned(x, by):
        by = by % 128
        return x if by == 0 else pltpu.roll(x, by, 1)

    within = lane & (STRIDE - 1)

    def outer(which, p, q):
        return turned(jnp.where(lane < 64, tile(which, p, 0), tile(which, p, 1)), STRIDE * q + HALO)

    def spot(which, group):
        return which, (group if which < 6 else 0)

    for group in range(TILES):
        for cp in loads[group]:
            cp.wait()
        for which in range(8 if group == 0 else 6):
            start = acc = outer(which, group * GROUP, 0)
            for q in range(1, GROUP):
                acc = jnp.where(lane >= STRIDE * q - HALO, outer(which, group * GROUP + q, q), acc)
            edges[which, group] = jnp.where(lane >= 128 - HALO, start, acc)

        for side in range(2):
            acc = None
            for which, width, to in PIECES:
                source = HALO if side == 0 else HALO - width
                x = turned(edges[spot(which, group)], to - source)
                acc = x if acc is None else jnp.where(within >= to, x, acc)
            msg_out[side, group] = acc

    pl.semaphore_wait(barrier, len(everyone))
    halos = [
        remote(msg_out.at[s], msg_in.at[1 - s], halo_send.at[s], halo_recv.at[1 - s], sides[s])
        for s in range(2)
    ]
    for cp in halos:
        cp.start()

    def share(on_core, group):
        part = pool.at[pl.ds(on_core * PART + GROUP * group, GROUP)]
        return remote(part, part, pool_send.at[group], pool_recv.at[group], sibling)

    def interior(p, carry):
        at = core * PART + p
        three_steps(
            lambda f, r, t: block(ens, (p, f), r, t), lambda f, r, t, x: put(pool, (at, f), r, t, x),
            hs, vs, us, cor_v, lambda r, t: block(fields, (0,), r, t), lambda r, t: block(fields, (2,), r, t),
            lambda step, r, t: block(pert, (p, step), r, t), 2,
        )
        return carry

    def interiors(group, carry):
        lax.fori_loop(GROUP * group, GROUP * group + GROUP, interior, 0)
        share(core, group).start()
        return carry

    lax.fori_loop(0, TILES, interiors, 0)

    for s in range(2):
        remote(msg_out.at[s], msg_in.at[s], halo_send.at[s], halo_recv.at[s], sides[s]).wait_recv()

    def edge_copy(on_core, group):
        part = edge.at[on_core, group]
        return remote(part, part, edge_sem.at[0, group], edge_sem.at[1, group], sibling)

    def edge_group(n, carry):
        for s in range(2):
            for which, width, at in PIECES:
                to = HALO - width if s == 0 else HALO
                x = turned(msg_in[s, n], to - at)
                inside = (within >= to) & (within < to + width)
                win[s, which, n] = jnp.where(inside, x, edges[which, n if which < 6 else 0])
            win[s, 5, n] = edges[5, n]
            three_steps(
                lambda f, r, t: block(win, (s, f, n), r, t), lambda f, r, t, x: put(half, (s, f), r, t, x),
                hs, vs, us, cor_v, lambda r, t: block(win, (s, 6, n), r, t),
                lambda r, t: block(win, (s, 7, n), r, t), lambda step, r, t: block(win, (s, 3 + step, n), r, t), 1,
            )
        for f in range(3):
            edge[core, n, f] = jnp.where((within >= HALO) & (within < 2 * HALO), half[0, f], half[1, f])
        edge_copy(core, n).start()
        return carry

    lax.fori_loop(0, TILES, edge_group, 0)
    for group in range(TILES):
        share(1 - core, group).wait_recv()
    for group in range(TILES):
        edge_copy(1 - core, group).wait_recv()

    def whole(i):
        on = jnp.where(i >= PART, 1, 0)
        p = i - on * PART
        group = lax.shift_right_logical(p, 2)
        back = 128 - HALO - STRIDE * (p - GROUP * group)
        out = []
        for f in range(3):
            x = pltpu.roll(edge[on, group, f], back, 1)
            low = jnp.where(lane < HALO, x, pool[i, f, :, 0:128])
            high = jnp.where(lane >= 128 - HALO, x, pool[i, f, :, 128:256])
            out.append((low, high))
        return out

    positions = (size + 1) // 2
    open_pos, far_pos = opened // 2, far // 2

    def split(pos):
        return 2 * pos + 1 == size

    def entry_at(pos, on_core):
        return 2 * pos if split(pos) else 2 * pos + on_core

    def rows(ref, pos, on_core):
        return ref.at[:, pl.ds(on_core * (LAT // 2), LAT // 2), :] if split(pos) else ref

    def landing(way, pos, on_core):
        i = entry_at(pos, on_core)
        if pos < far_pos:
            return first.at[way, i]
        return rows(slots.at[CHIP + way * CAPACITY + i], pos, on_core)

    def ring_copy(way, pos):
        return remote(
            rows(stage.at[way, pos], pos, core), landing(way, pos, core),
            ring_send.at[way, pos], ring_recv.at[way, pos], ring[way],
        )

    def mirror_copy(way, pos, on_core):
        ref = landing(way, pos, on_core)
        return remote(ref, ref, mir_send.at[way, pos], mir_recv.at[way, pos], sibling)

    for pos in range(open_pos):
        for way in range(2):
            parts = whole(plan[way * CAPACITY + entry_at(pos, core)])
            for f in range(3):
                stage[way, pos, f, :, 0:128], stage[way, pos, f, :, 128:256] = parts[f]
            ring_copy(way, pos).start()

    for group in range(TILES):
        share(core, group).wait_send()

    def complete(i, carry):
        parts = whole(i)
        for f in range(3):
            pool[i, f, :, 0:128], pool[i, f, :, 128:256] = parts[f]
        lo = fields[0, :, 0:128] - parts[2][0]
        hi = fields[0, :, 128:256] - parts[2][1]
        term = fields[1, :, 0:128] * lo * lo + fields[1, :, 128:256] * hi * hi
        misfit[i] = jnp.sum(term.reshape(LAT // 8, 8, 128), axis=0)
        return carry

    lax.fori_loop(0, CHIP, complete, 0)
    keep = [pltpu.make_async_copy(pool, slots.at[pl.ds(0, CHIP)], out_sem.at[0])]
    keep[0].start()

    total = jnp.sum(jnp.sum(misfit[pl.ds(core * PART, PART)], axis=1), axis=1, keepdims=True)
    small = lax.broadcasted_iota(jnp.int32, (PART, 128), 1)
    which = lax.broadcasted_iota(jnp.int32, (PART, 128), 0)
    line = jnp.sum(jnp.where(small == which, total, 0.0), axis=0, keepdims=True)
    zbuf[lon_z] = jnp.broadcast_to(line, (8, 128))
    z_copies = [
        remote(zbuf.at[lon_z], zbuf.at[lon_z], z_send.at[k], z_recv.at[k], z_peers[k]) for k in range(3)
    ]
    for cp in z_copies:
        cp.start()

    for k in range(3):
        z_copies[k].wait_send()
        z_copies[k].wait_recv()
    xbuf[lon_x] = ((zbuf[0] + zbuf[1]) + zbuf[2]) + zbuf[3]
    x_copies = [
        remote(xbuf.at[lon_x], xbuf.at[lon_x], x_send.at[k], x_recv.at[k], x_peers[k]) for k in range(3)
    ]
    for cp in x_copies:
        cp.start()
    for cp in x_copies:
        cp.wait_send()
        cp.wait_recv()
    lwbuf[member] = ((xbuf[0] + xbuf[1]) + xbuf[2]) + xbuf[3]
    m_copies = [
        remote(lwbuf.at[member], lwbuf.at[member], m_send.at[k], m_recv.at[k], m_peers[k]) for k in range(7)
    ]
    for cp in m_copies:
        cp.start()

    for pos in range(far_pos):
        for way in range(2):
            ring_copy(way, pos).wait_recv()
            mirror_copy(way, pos, core).start()
    for pos in range(far_pos):
        for way in range(2):
            mirror_copy(way, pos, 1 - core).wait_recv()
    for way in range(2):
        cp = pltpu.make_async_copy(
            first.at[way], slots.at[pl.ds(CHIP + way * CAPACITY, far)], out_sem.at[1 + way]
        )
        cp.start()
        keep.append(cp)
    for pos in range(open_pos, positions):
        for way in range(2):
            idx = plan[way * CAPACITY + entry_at(pos, core)]
            own = pool[jnp.minimum(idx, CHIP - 1)]
            passed = first[way, jnp.clip(idx - CHIP, 0, far - 1)]
            stage[way, pos] = jnp.where(idx < CHIP, own, passed)
            ring_copy(way, pos).start()
    for pos in range(far_pos, positions):
        for way in range(2):
            ring_copy(way, pos).wait_recv()
            mirror_copy(way, pos, core).start()

    for cp in m_copies:
        cp.wait_send()
        cp.wait_recv()
    lw_out[...] = lwbuf[...]
    for cp in halos:
        cp.wait_send()
    for group in range(TILES):
        edge_copy(core, group).wait_send()
    for pos in range(positions):
        for way in range(2):
            ring_copy(way, pos).wait_send()
    for pos in range(positions):
        for way in range(2):
            mirror_copy(way, pos, core).wait_send()
            if pos >= far_pos:
                mirror_copy(way, pos, 1 - core).wait_recv()
    for cp in keep:
        cp.wait()


def run_cycle(level, number, plan, ensemble, perturbation, observed, precision, nudging):
    anywhere = pl.BlockSpec(memory_space=pltpu.HBM)
    dma = pltpu.SemaphoreType.DMA
    most = (level[0] + 1) // 2
    return pl.pallas_call(
        functools.partial(cycle_kernel, level),
        out_shape=(
            jax.ShapeDtypeStruct((SLOTS, 3, LAT, CLON), F32),
            jax.ShapeDtypeStruct((8, 8, 128), F32),
        ),
        in_specs=[pl.BlockSpec(memory_space=pltpu.SMEM)] + [anywhere] * 5,
        out_specs=(anywhere, pl.BlockSpec(memory_space=pltpu.VMEM)),
        scratch_shapes=[
            pltpu.VMEM((PART, 3, LAT, CLON), F32),
            pltpu.VMEM((PART, 3, LAT, CLON), F32),
            pltpu.VMEM((3, LAT, CLON), F32),
            pltpu.VMEM((LAT, 128), F32),
            pltpu.VMEM((CHIP, 3, LAT, CLON), F32),
            pltpu.VMEM((2, level[1], 3, LAT, CLON), F32),
            pltpu.VMEM((2, most, 3, LAT, CLON), F32),
            pltpu.VMEM((2, 3, LAT, 128), F32),
            pltpu.VMEM((2, 3, LAT, 128), F32),
            pltpu.VMEM((8, TILES, LAT, 128), F32),
            pltpu.VMEM((2, 8, TILES, LAT, 128), F32),
            pltpu.VMEM((2, 3, LAT, 128), F32),
            pltpu.VMEM((2, TILES, 3, LAT, 128), F32),
            pltpu.VMEM((2, 2, LAT + 16, 128), F32),
            pltpu.VMEM((2, 2, LAT + 16, 128), F32),
            pltpu.VMEM((2, 2, LAT + 16, 128), F32),
            pltpu.VMEM((CHIP, 8, 128), F32),
            pltpu.VMEM((4, 8, 128), F32),
            pltpu.VMEM((4, 8, 128), F32),
            pltpu.VMEM((8, 8, 128), F32),
            dma((2, 3)), dma((3,)), dma((2,)), dma((2,)), dma((TILES,)), dma((TILES,)), dma((2, TILES)),
            dma((2, most)), dma((2, most)), dma((2, most)), dma((2, most)), dma((3,)),
            dma((3,)), dma((3,)), dma((3,)), dma((3,)), dma((7,)), dma((7,)),
        ],
        compiler_params=pltpu.CompilerParams(
            collective_id=number, has_side_effects=True, vmem_limit_bytes=50 * 2**20
        ),
    )(plan, ensemble, perturbation, observed, precision, nudging)


def resample_kernel(plan, lw_ref, slots, weights_ref, analysis, held, in_sem, out_sem):
    ins = [
        pltpu.make_async_copy(slots.at[plan[GATHER_AT + j]], held.at[j], in_sem.at[j]) for j in range(PART)
    ]
    outs = [pltpu.make_async_copy(held.at[j], analysis.at[j], out_sem.at[j]) for j in range(PART)]
    for cp in ins:
        cp.start()
    lane = lax.broadcasted_iota(jnp.int32, (8, 8, 128), 2)
    logw = jnp.where(lane < PART, lw_ref[...] * (-2.0 / (LAT * CLON * 16)), -jnp.inf)
    top = jnp.max(jnp.max(logw, axis=0), axis=1, keepdims=True)
    e = jnp.exp(logw - top[None])
    whole = jnp.sum(jnp.sum(e, axis=0), axis=1, keepdims=True)
    own = jnp.where(
        lax.broadcasted_iota(jnp.int32, (8, 8, 128), 0) == lax.axis_index("member"), e, 0.0
    )
    row = jnp.sum(own, axis=0) / whole
    weights_ref[...] = row[0, :PART]
    for j in range(PART):
        ins[j].wait()
        outs[j].start()
    for cp in outs:
        cp.wait()


def resample(plan, lw, slots):
    return pl.pallas_call(
        resample_kernel,
        out_shape=(
            jax.ShapeDtypeStruct((PART,), F32),
            jax.ShapeDtypeStruct((PART, 3, LAT, CLON), F32),
        ),
        in_specs=[
            pl.BlockSpec(memory_space=pltpu.SMEM),
            pl.BlockSpec(memory_space=pltpu.VMEM),
            pl.BlockSpec(memory_space=pltpu.HBM),
        ],
        out_specs=(pl.BlockSpec(memory_space=pltpu.VMEM), pl.BlockSpec(memory_space=pltpu.HBM)),
        scratch_shapes=[
            pltpu.VMEM((PART, 3, LAT, CLON), F32),
            pltpu.SemaphoreType.DMA((PART,)),
            pltpu.SemaphoreType.DMA((PART,)),
        ],
    )(plan, lw, slots)


def body(ensemble, perturbation, observed, precision, nudging, ancestors):
    plan, level = make_plan(ancestors)
    operands = (plan, ensemble, perturbation, observed, precision, nudging)
    branches = [functools.partial(run_cycle, form, n) for n, form in enumerate(LEVELS)]
    if len(branches) == 1:
        slots, lw = branches[0](*operands)
    else:
        slots, lw = lax.switch(level.reshape(()), branches, *operands)
    weights, analysis = resample(plan, lw, slots)
    return weights, analysis


def solution(mesh):
    placed = (
        P("member", None, None, "lon"),
        P("member", None, None, "lon"),
        P(None, "lon"),
        P(None, "lon"),
        P(None, "lon"),
        P(),
    )
    return jax.shard_map(
        body,
        mesh=mesh,
        in_specs=placed,
        out_specs=(P("member"), P("member", None, None, "lon")),
        check_vma=False,
    )
```
